256 devices in a mesh: fft: 32 (over z, x_lo, core), grp: 8 (over y, x_hi).
Axes of the slice: x: 4 (x_hi: 2, x_lo: 2; x = x_hi * 2 + x_lo), y: 4, z: 8, core: 2. Of those that a mesh axis runs over, the one named last changes fastest.
Arguments:
- psi_valence: bfloat16 [16, 64, 4096], P(None, 'fft'), may hold values from -6 to 6
- psi_conduction: bfloat16 [384, 64, 4096], P(None, 'fft'), may hold values from -6 to 6
- energy_valence: float32 [16], replicated, may hold values from -6 to -0.5
- energy_conduction: float32 [384], replicated, may hold values from 0.5 to 8
- pair_valence: int32 [320], P('grp'), may hold values from 0 to 15
- pair_conduction: int32 [320], P('grp'), may hold values from 0 to 383
- g_index: int32 [6144], replicated, may hold values from 0 to 262143, as said below
Outputs:
- chi_real: float32 [6144, 6144], P('fft', 'grp')
- chi_imag: float32 [6144, 6144], P('fft', 'grp')
The draws below stay inside these ranges and needn't reach their ends.
Inputs may be any that keep to these rules, and one draw needn't show every extreme that they name: `g_index`: the 6144 entries are distinct grid points in flat order a * 64 * 64 + b * 64 + c.
All inputs are finite; a program needn't handle non-finite values.
Results may differ from the reference program's by a relative error of at most 0.0041.
Values may be sent and summed in bfloat16 or wider, within the bound.
A program may use at most 128 MiB of HBM per device.

```python
import jax
import jax.numpy as jnp
from jax import lax

NG = 64
V = 16
C = 384
NGV = 6144
ALL_PAIRS = 320


def draw_g_index(key, part):
    key = jax.random.fold_in(key, 7)
    perm_key, order_key = jax.random.split(key)
    grid_total = NG * NG * NG
    interior = jax.random.permutation(perm_key, grid_total - 2)[:NGV - 2].astype(jnp.int32) + 1
    chosen = jnp.concatenate([jnp.array([0, grid_total - 1], dtype=jnp.int32), interior])
    return jax.random.permutation(order_key, chosen).astype(jnp.int32)


def plant(entries, rng, least, high):
    longest = entries.shape.index(max(entries.shape))
    spots = []
    for shift in (0, 1):
        where = [jax.random.randint(jax.random.fold_in(rng, axis), (), 0, length) for axis, length in enumerate(entries.shape)]
        where[longest] = (where[longest] + shift) % entries.shape[longest]
        spots.append(tuple(where))
    return entries.at[spots[0]].set(least).at[spots[1]].set(high)


def level_of(key, extent, cuts, low, top_value):
    level = 1.0
    for dim, parts in cuts:
        draws = jax.random.uniform(jax.random.fold_in(jax.random.fold_in(key, 6), dim), (parts,), jnp.float32, low / len(cuts), top_value / len(cuts))
        level = level * jnp.repeat(jnp.exp(draws), extent[dim] // parts).reshape((-1,) + (1,) * (len(extent) - 1 - dim))
    return level


def centred(key, dims, width, limit, pieces=(), held_as=jnp.bfloat16):
    result = jax.random.normal(key, dims, jnp.float32) * width
    if len(pieces) > 0:
        result = level_of(key, dims, pieces, -0.22, 0.18) * result
    return jnp.clip(result, min=-limit, max=limit).astype(held_as)


def setup_inputs(seed: int = 0) -> dict:
    key_list = jax.random.split(jax.random.key(seed), 8)
    psi_valence = centred(key_list[0], (V, NG, NG * NG), 1.0, 6.0, ((1, 32),))
    psi_conduction = centred(key_list[1], (C, NG, NG * NG), 1.0, 6.0, ((1, 32),))
    energy_valence = jnp.clip(jax.random.uniform(key_list[2], (V,), jnp.float32, -6.0, -0.5), -6.0, -0.5)
    energy_conduction = jnp.clip(jax.random.uniform(key_list[3], (C,), jnp.float32, 0.5, 8.0), 0.5, 8.0)
    pair_valence = plant(jax.random.randint(key_list[4], (ALL_PAIRS,), 0, V), jax.random.fold_in(key_list[4], 1), 0, V - 1).astype(jnp.int32)
    pair_conduction = plant(jax.random.randint(key_list[5], (ALL_PAIRS,), 0, C), jax.random.fold_in(key_list[5], 1), 0, C - 1).astype(jnp.int32)
    g_index = draw_g_index(jax.random.fold_in(key_list[7], 71), 0)
    return {"psi_valence": psi_valence, "psi_conduction": psi_conduction, "energy_valence": energy_valence, "energy_conduction": energy_conduction, "pair_valence": pair_valence, "pair_conduction": pair_conduction, "g_index": g_index}


def reference(psi_valence, psi_conduction, energy_valence, energy_conduction, pair_valence, pair_conduction, g_index):
    weight = 2.0 / (energy_conduction[pair_conduction] - energy_valence[pair_valence])
    factor = jnp.sqrt(weight) * ALL_PAIRS ** (-0.25) * NG ** (-1.5)

    def transform(band_pair):
        density = psi_valence[band_pair[0]].astype(jnp.float32) * psi_conduction[band_pair[1]].astype(jnp.float32)
        density = density.reshape(NG, NG, NG)
        spectrum = jnp.fft.fftn(density).reshape(-1)[g_index]
        return (jnp.real(spectrum), jnp.imag(spectrum))
    sphere_real, sphere_imag = lax.map(transform, (pair_valence, pair_conduction))
    scaled_real = (sphere_real * factor[:, None]).astype(jnp.bfloat16)
    scaled_imag = (sphere_imag * factor[:, None]).astype(jnp.bfloat16)
    stack_sum = jnp.concatenate([scaled_real, scaled_imag], 0)
    left_cross = jnp.concatenate([scaled_real, -scaled_imag], 0)
    right_cross = jnp.concatenate([scaled_imag, scaled_real], 0)
    chi_real = -jnp.dot(stack_sum.T, stack_sum, preferred_element_type=jnp.float32)
    chi_imag = jnp.dot(left_cross.T, right_cross, preferred_element_type=jnp.float32)
    return (chi_real, chi_imag)
```

```python
import functools
import math

import jax
import jax.numpy as jnp
import ml_dtypes
import numpy as np
from jax import lax
from jax.experimental import pallas as pl
from jax.experimental.pallas import tpu as pltpu
from jax.sharding import PartitionSpec as P

NG = 64
HALF_C = 34
KEYS = HALF_C * NG
PAIRS = 40
BOTH = 2 * PAIRS
CHIPS = 16
CHIP_POINTS = 384
BF16 = jnp.bfloat16
F32 = jnp.float32
MESH = pl.DeviceIdType.MESH


def split_table(table):
    high = table.astype(ml_dtypes.bfloat16)
    low = (table - high.astype(np.float64)).astype(ml_dtypes.bfloat16)
    return high, low


def table_z():
    c, z = np.arange(33)[:, None], np.arange(NG)[None, :]
    angle = 2 * np.pi * ((c * z) % NG) / NG
    table = np.zeros((HALF_C, 4, 2, 4, NG))
    for y in range(4):
        table[:33, y, 0, y] = np.cos(angle)
        table[:33, y, 1, y] = -np.sin(angle)
    high, low = split_table(table.reshape(HALF_C * 8, 4 * NG))
    return np.concatenate([high, high, low], 1)


def table_y():
    y, b = np.arange(NG)[:, None], np.arange(NG)[None, :]
    angle = 2 * np.pi * ((y * b) % NG) / NG
    table = np.zeros((NG, 2, 2, NG))
    table[:, 0, 0], table[:, 0, 1] = np.cos(angle), -np.sin(angle)
    table[:, 1, 0], table[:, 1, 1] = np.sin(angle), np.cos(angle)
    high, low = split_table(table.reshape(2 * NG, 2 * NG))
    return np.concatenate([high, high, low], 0)


def table_x():
    angle = 2 * np.pi * np.arange(NG) / NG
    table = np.zeros((8, NG), np.float32)
    table[0], table[1] = np.cos(angle), np.sin(angle)
    return table


def split(x):
    high = x.astype(BF16)
    return high, (x - high.astype(F32)).astype(BF16)


def dot(a, b, contract, precision=None):
    return lax.dot_general(
        a, b, (contract, ((), ())), precision=precision, preferred_element_type=F32
    )


def front_kernel(
    total_pairs,
    pair_c, pair_v, energy_c, energy_v, plane,
    psi_c, psi_v, wz, wy, wx, g_index,
    out,
    band_v, band_c, density, z_part, y_part, sem,
):
    copy_v = pltpu.make_async_copy(psi_v, band_v, sem.at[1])
    copy_v.start()

    def fetch(p, _):
        pltpu.make_async_copy(psi_c.at[pair_c[p]], band_c.at[p], sem.at[0]).start()
        return 0

    lax.fori_loop(0, PAIRS, fetch, 0)

    row = lax.broadcasted_iota(jnp.int32, (BOTH, 128), 0)
    row = jnp.where(row >= PAIRS, row - PAIRS, row)

    def gaps(p, gap):
        return jnp.where(row == p, energy_c[pair_c[p]] - energy_v[pair_v[p]], gap)

    gap = lax.fori_loop(0, PAIRS, gaps, jnp.ones((BOTH, 128), F32))
    factor = jnp.sqrt(2.0 / gap) * (total_pairs ** (-0.25) * NG ** (-1.5))

    copy_v.wait()
    pltpu.make_async_copy(psi_c.at[pl.ds(0, PAIRS)], band_c, sem.at[0]).wait()

    def multiply(p, _):
        start = pl.multiple_of(p * NG, NG)
        density[pl.ds(start, NG), :] = band_v[pair_v[p]].astype(F32) * band_c[p].astype(F32)
        return 0

    lax.fori_loop(0, PAIRS, multiply, 0)

    def along_z(i, _):
        lines = []
        for t in range(2):
            lines.append(jnp.concatenate(
                [density[pl.ds(4 * i + 2 * t + x, PAIRS, stride=NG), :] for x in range(2)], 0
            ))
        high, low = split(jnp.concatenate(lines, 1))
        lines = jnp.concatenate([high, low, high], 1)
        result = dot(wz[...], lines, ((1,), (1,)))
        start = pl.multiple_of(8 * i, 8)
        z_part[:, pl.ds(start, 8), 0:BOTH] = result.reshape(HALF_C, 8, BOTH)
        return 0

    lax.fori_loop(0, NG // 4, along_z, 0)

    lane = lax.broadcasted_iota(jnp.int32, (BOTH, 128), 1)

    def along_y(k, most):
        lines = jnp.concatenate([z_part[2 * k + c].T[0:BOTH] for c in range(2)], 0)
        high, low = split(lines)
        result = dot(jnp.concatenate([high, low, high], 1), wy[...], ((1,), (0,)))
        first, second = result[0:BOTH], result[BOTH:]
        real = jnp.where(lane < NG, first, pltpu.roll(second, NG, 1)) * factor
        imag = jnp.where(lane < NG, pltpu.roll(first, NG, 1), second) * factor
        start = pl.multiple_of(128 * k, 128)
        for i, part in enumerate(split(real) + split(imag)):
            place = (0, 2, 1, 3)[i] * BOTH
            y_part[place:place + BOTH, pl.ds(start, 128)] = part
        size = jnp.abs(real) + jnp.abs(imag)
        return jnp.maximum(most, size[0:PAIRS] + size[PAIRS:])

    most = lax.fori_loop(0, HALF_C // 2, along_y, jnp.zeros((PAIRS, 128), F32))
    most = jnp.max(jnp.max(most, 0, keepdims=True), 1, keepdims=True)
    level = jnp.floor(jnp.log2(jnp.maximum(most, 1e-30) * 1.001)) + 1.0
    level_rows = jnp.broadcast_to(level, (8, 128))
    up = jnp.exp2(15.0 - level)

    x0 = plane[0]
    half_lane = lax.broadcasted_iota(jnp.int32, (PAIRS, 128), 1) < NG
    key_row = lax.broadcasted_iota(jnp.int16, (KEYS, CHIP_POINTS), 0)
    turn_row = lax.broadcasted_iota(jnp.int32, (NG, 2 * CHIP_POINTS), 0)

    def select(j, _):
        g = g_index[0:1, pl.ds(pl.multiple_of(j * CHIP_POINTS, 128), CHIP_POINTS)]
        a, b, c = g >> 12, (g >> 6) & 63, g & 63
        mirror = c > 32
        a = jnp.where(mirror, (NG - a) & 63, a)
        b = jnp.where(mirror, (NG - b) & 63, b)
        c = jnp.where(mirror, NG - c, c)
        key = (c * NG + b).astype(jnp.int16)
        chosen = jnp.where(key_row == key, BF16(1), BF16(0))
        picked = dot(y_part[...], chosen, ((1,), (0,)))
        picked = picked[0:2 * BOTH] + picked[2 * BOTH:]
        re0, re1, im0, im1 = (picked[i * PAIRS:(i + 1) * PAIRS] for i in range(4))
        turns = jnp.concatenate([(a * x0) & 63, (a * (x0 + 1)) & 63], 1)
        phase = dot(wx[...], (turn_row == turns).astype(F32), ((1,), (0,)), lax.Precision.HIGHEST)
        cos0, cos1 = phase[0:1, 0:CHIP_POINTS], phase[0:1, CHIP_POINTS:]
        sin0, sin1 = phase[1:2, 0:CHIP_POINTS], phase[1:2, CHIP_POINTS:]
        sign = jnp.where(mirror, -up, up)
        real = (cos0 * re0 + sin0 * im0 + cos1 * re1 + sin1 * im1) * up
        imag = (cos0 * im0 - sin0 * re0 + cos1 * im1 - sin1 * re1) * sign
        real, imag = jnp.floor(real + 0.5), jnp.floor(imag + 0.5)
        middle_re, middle_im = real[:, 128:256], imag[:, 128:256]
        for core in range(2):
            if core == 0:
                middle = jnp.where(half_lane, middle_re, pltpu.roll(middle_im, NG, 1))
            else:
                middle = jnp.where(half_lane, pltpu.roll(middle_re, NG, 1), middle_im)
            lanes = slice(256 * core, 256 * core + 128)
            slab = jnp.concatenate([real[:, lanes], imag[:, lanes], middle, level_rows], 0)
            out[core, j] = slab.astype(jnp.int32).astype(jnp.int16)
        return 0

    lax.fori_loop(0, CHIPS, select, 0)


def front(pair_c, pair_v, energy_c, energy_v, plane, psi_c, psi_v, g_index, total_pairs):
    smem = pl.BlockSpec(memory_space=pltpu.SMEM)
    vmem = pl.BlockSpec(memory_space=pltpu.VMEM)
    anywhere = pl.BlockSpec(memory_space=pl.ANY)
    return pl.pallas_call(
        functools.partial(front_kernel, total_pairs),
        out_shape=jax.ShapeDtypeStruct((2, CHIPS, 128, 128), jnp.int16),
        in_specs=[smem] * 5 + [anywhere] * 2 + [vmem] * 4,
        out_specs=vmem,
        scratch_shapes=[
            pltpu.VMEM(psi_v.shape, BF16),
            pltpu.VMEM((PAIRS, NG, 128), BF16),
            pltpu.VMEM((PAIRS * NG, 128), F32),
            pltpu.VMEM((HALF_C, 128, 128), F32),
            pltpu.VMEM((4 * BOTH, KEYS), BF16),
            pltpu.SemaphoreType.DMA((2,)),
        ],
        compiler_params=pltpu.CompilerParams(vmem_limit_bytes=40 * 1024 * 1024),
    )(
        pair_c, pair_v, energy_c, energy_v, plane, psi_c, psi_v,
        jnp.asarray(table_z()), jnp.asarray(table_y()), jnp.asarray(table_x()), g_index,
    )


def exchange_kernel(
    q, chi_real, chi_imag,
    core_in, chip_out, chip_in, block, z_blocks, row_blocks, col_blocks,
    core_send, core_recv, chip_send, chip_recv, z_send, z_recv,
    row_send, row_recv, plane_send, plane_recv, relay_send, relay_recv,
):
    f, g = lax.axis_index("fft"), lax.axis_index("grp")
    core, chip, z = f % 2, f // 2, f // 4
    x = chip % 2
    sibling = f + 1 - 2 * core

    def remote(src, dst, send, recv, to):
        return pltpu.make_async_remote_copy(
            src_ref=src, dst_ref=dst, send_sem=send, recv_sem=recv,
            device_id=to, device_id_type=MESH,
        )

    barrier = pltpu.get_barrier_semaphore()
    pl.semaphore_signal(barrier, 1, device_id=(sibling, g), device_id_type=MESH)

    def greet_chip(k, _):
        to = ((2 * chip + 2 * k) % 32 + core, g)
        pl.semaphore_signal(barrier, 1, device_id=to, device_id_type=MESH)
        return 0

    lax.fori_loop(1, CHIPS, greet_chip, 0)

    def greet_plane(k, _):
        to = (z * 4 + (k % 2) * 2 + core, (g + k // 2) % 8)
        pl.semaphore_signal(barrier, 1, device_id=to, device_id_type=MESH)
        return 0

    lax.fori_loop(2, 16, greet_plane, 0)
    pl.semaphore_wait(barrier, 30)

    def to_sibling(j):
        return remote(q.at[1 - core, j], core_in.at[j], core_send.at[j], core_recv.at[j], (sibling, g))

    def send_core(k, _):
        to_sibling((chip + k) % CHIPS).start()
        return 0

    lax.fori_loop(1, CHIPS + 1, send_core, 0)

    tail = lax.broadcasted_iota(jnp.int32, (128, 128), 0) >= 120

    def to_chip(j):
        return remote(
            chip_out.at[j], chip_in.at[chip], chip_send.at[j], chip_recv.at[chip], (2 * j + core, g)
        )

    def add_core(k, _):
        j = (chip + k) % CHIPS
        to_sibling(j).wait_recv()
        own, other = q[core, j].astype(jnp.int32).astype(F32), core_in[j].astype(jnp.int32).astype(F32)
        own_level, other_level = own[120:121], other[120:121]
        level = jnp.maximum(own_level, other_level) + 1.0
        total = own * jnp.exp2(own_level - level) + other * jnp.exp2(other_level - level)
        total = jnp.where(tail, level, jnp.floor(total + 0.5))
        chip_out[j] = total.astype(jnp.int32).astype(jnp.int16)

        @pl.when(k < CHIPS)
        def _():
            to_chip(j).start()

        return 0

    lax.fori_loop(1, CHIPS + 1, add_core, 0)

    def scaled(slab):
        slab = slab.astype(jnp.int32).astype(F32)
        return slab * jnp.exp2(slab[120:121] - 15.0)

    def add_chip(k, total):
        j = (chip + k) % CHIPS
        remote(
            chip_out.at[j], chip_in.at[j], chip_send.at[j], chip_recv.at[j], (2 * j + core, g)
        ).wait_recv()
        return total + scaled(chip_in[j])

    total = lax.fori_loop(1, CHIPS, add_chip, scaled(chip_out[chip]))
    block[...] = jnp.where(tail, 0.0, total).astype(BF16)

    def to_z(k):
        other = (z + k) % 8
        return remote(
            block, z_blocks.at[z], z_send.at[other], z_recv.at[z], (other * 4 + x * 2 + core, g)
        )

    def to_row(k):
        other = (g + k) % 8
        return remote(block, row_blocks.at[g], row_send.at[other], row_recv.at[g], (f, other))

    def send_block(k, _):
        to_z(k).start()
        to_row(k).start()
        return 0

    lax.fori_loop(1, 8, send_block, 0)
    z_blocks[z] = block[...]
    row_blocks[g] = block[...]

    def to_plane(layer, to_x):
        return remote(
            z_blocks.at[layer], col_blocks.at[core, x, g],
            plane_send.at[layer, to_x], plane_recv.at[x, g], (z * 4 + to_x * 2 + core, layer),
        )

    def stays(layer, to_x):
        return jnp.logical_and(layer == g, to_x == x)

    def spread(k, _):
        layer = (z + (k + 1) // 2 * (1 - 2 * (k % 2)) + 8) % 8

        @pl.when(k > 0)
        def _():
            remote(
                block, z_blocks.at[layer], z_send.at[layer], z_recv.at[layer],
                (layer * 4 + x * 2 + core, g),
            ).wait_recv()

        for to_x in range(2):
            @pl.when(stays(layer, to_x))
            def _():
                col_blocks[core, x, g] = z_blocks[layer]

            @pl.when(jnp.logical_not(stays(layer, to_x)))
            def _():
                to_plane(layer, to_x).start()

        return 0

    lax.fori_loop(0, 8, spread, 0)

    def relay(side, from_x, from_g):
        return remote(
            col_blocks.at[side, from_x, from_g], col_blocks.at[side, from_x, from_g],
            relay_send.at[from_x, from_g], relay_recv.at[from_x, from_g], (sibling, g),
        )

    def pass_on(k, _):
        from_x, from_g = (x + k) % 2, (g + k // 2) % 8

        @pl.when(k > 0)
        def _():
            remote(
                z_blocks.at[0], col_blocks.at[core, from_x, from_g],
                plane_send.at[0, 0], plane_recv.at[from_x, from_g],
                (z * 4 + from_x * 2 + core, from_g),
            ).wait_recv()

        relay(core, from_x, from_g).start()
        return 0

    lax.fori_loop(0, 16, pass_on, 0)

    def row_arrives(k, _):
        other = (g + k) % 8
        remote(
            block, row_blocks.at[other], row_send.at[other], row_recv.at[other], (f, other)
        ).wait_recv()
        return 0

    lax.fori_loop(1, 8, row_arrives, 0)

    def relay_arrives(k, _):
        relay(1 - core, k % 2, k // 2).wait_recv()
        return 0

    lax.fori_loop(0, 16, relay_arrives, 0)

    half_lane = lax.broadcasted_iota(jnp.int32, (8 * PAIRS, 128), 1) < NG

    def gather(read):
        blocks = [read(i).astype(F32) for i in range(8)]
        return tuple(
            jnp.concatenate([b[s * PAIRS:(s + 1) * PAIRS] for b in blocks], 0) for s in range(3)
        )

    real, imag, middle = gather(lambda i: row_blocks[i])
    full = jnp.concatenate([real, imag], 0).astype(BF16)
    half = jnp.concatenate([middle, pltpu.roll(middle, NG, 1)], 0)[:, 0:NG].astype(BF16)
    full_row = pl.multiple_of(core * NG, NG)
    half_row = pl.multiple_of((1 - core) * 128, NG)
    for side in range(2):
        real0, imag0, middle0 = gather(lambda i: col_blocks[0, side, i])
        real2, imag2, middle2 = gather(lambda i: col_blocks[1, side, i])
        real1 = jnp.where(half_lane, middle0, pltpu.roll(middle2, NG, 1))
        imag1 = jnp.where(half_lane, pltpu.roll(middle0, NG, 1), middle2)
        real = jnp.concatenate([real0, real1, real2], 1)
        imag = jnp.concatenate([imag0, imag1, imag2], 1)
        right_sum = jnp.concatenate([real, imag], 0).astype(BF16)
        right_cross = jnp.concatenate([imag, -real], 0).astype(BF16)
        lanes = slice(side * CHIP_POINTS, (side + 1) * CHIP_POINTS)
        for left, rows in ((full, pl.ds(full_row, 128)), (half, pl.ds(half_row, NG))):
            chi_real[rows, lanes] = -dot(left, right_sum, ((0,), (0,)))
            chi_imag[rows, lanes] = dot(left, right_cross, ((0,), (0,)))

    def drain_chips(k, _):
        to_sibling((chip + k) % CHIPS).wait_send()

        @pl.when(k < CHIPS)
        def _():
            to_chip((chip + k) % CHIPS).wait_send()

        return 0

    lax.fori_loop(1, CHIPS + 1, drain_chips, 0)

    def drain_blocks(k, _):
        to_z(k).wait_send()
        to_row(k).wait_send()
        return 0

    lax.fori_loop(1, 8, drain_blocks, 0)

    def drain_plane(k, _):
        @pl.when(jnp.logical_not(stays(k // 2, k % 2)))
        def _():
            to_plane(k // 2, k % 2).wait_send()

        relay(core, k % 2, k // 2).wait_send()
        return 0

    lax.fori_loop(0, 16, drain_plane, 0)


def exchange(q, rows, columns):
    vmem = pl.BlockSpec(memory_space=pltpu.VMEM)
    dma = pltpu.SemaphoreType.DMA
    slabs = pltpu.VMEM((CHIPS, 128, 128), jnp.int16)
    blocks = pltpu.VMEM((8, 128, 128), BF16)
    shape = jax.ShapeDtypeStruct((rows, columns), F32)
    return pl.pallas_call(
        exchange_kernel,
        out_shape=(shape, shape),
        in_specs=[vmem],
        out_specs=(vmem, vmem),
        scratch_shapes=[
            slabs, slabs, slabs,
            pltpu.VMEM((128, 128), BF16),
            blocks, blocks,
            pltpu.VMEM((2, 2, 8, 128, 128), BF16),
            dma((CHIPS,)), dma((CHIPS,)), dma((CHIPS,)), dma((CHIPS,)),
            dma((8,)), dma((8,)), dma((8,)), dma((8,)),
            dma((8, 2)), dma((2, 8)), dma((2, 8)), dma((2, 8)),
        ],
        compiler_params=pltpu.CompilerParams(
            collective_id=0, has_side_effects=True, vmem_limit_bytes=40 * 1024 * 1024
        ),
    )(q)


def per_device(
    psi_valence,
    psi_conduction,
    energy_valence,
    energy_conduction,
    pair_valence,
    pair_conduction,
    g_index,
):
    def tiles(psi):
        bands = psi.shape[0]
        return psi.reshape(bands, 2, 32, 128).transpose(0, 2, 1, 3).reshape(bands, NG, 128)

    plane = (2 * lax.axis_index("fft")).astype(jnp.int32).reshape(1)
    slabs = front(
        pair_conduction, pair_valence, energy_conduction, energy_valence, plane,
        tiles(psi_conduction), tiles(psi_valence), g_index.reshape(1, -1),
        PAIRS * lax.axis_size("grp"),
    )
    points = g_index.shape[0]
    return exchange(slabs, points // lax.axis_size("fft"), points // lax.axis_size("grp"))


def solution(mesh):
    placed = (P(None, "fft", None), P(None, "fft", None), P(), P(), P("grp"), P("grp"), P())
    return jax.shard_map(
        per_device,
        mesh=mesh,
        in_specs=placed,
        out_specs=(P("fft", "grp"), P("fft", "grp")),
        check_vma=False,
    )
```

```python
import functools
import math

import jax
import jax.numpy as jnp
import ml_dtypes
import numpy as np
from jax import lax
from jax.experimental import pallas as pl
from jax.experimental.pallas import tpu as pltpu
from jax.sharding import PartitionSpec as P

NG = 64
HALF_C = 34
KEYS = HALF_C * NG
PAIRS = 40
BOTH = 2 * PAIRS
CHIPS = 16
CHIP_POINTS = 384
WIDE = 2 * CHIP_POINTS
BF16 = jnp.bfloat16
F32 = jnp.float32
MESH = pl.DeviceIdType.MESH


def split_table(table):
    high = table.astype(ml_dtypes.bfloat16)
    low = (table - high.astype(np.float64)).astype(ml_dtypes.bfloat16)
    return high, low


def table_z():
    c, z = np.arange(33)[:, None], np.arange(NG)[None, :]
    angle = 2 * np.pi * ((c * z) % NG) / NG
    table = np.zeros((HALF_C, 4, 2, 4, NG))
    for y in range(4):
        table[:33, y, 0, y] = np.cos(angle)
        table[:33, y, 1, y] = -np.sin(angle)
    high, low = split_table(table.reshape(HALF_C * 8, 4 * NG))
    return np.concatenate([high, high, low], 1)


def table_y():
    y, b = np.arange(NG)[:, None], np.arange(NG)[None, :]
    angle = 2 * np.pi * ((y * b) % NG) / NG
    table = np.zeros((NG, 2, 2, NG))
    table[:, 0, 0], table[:, 0, 1] = np.cos(angle), -np.sin(angle)
    table[:, 1, 0], table[:, 1, 1] = np.sin(angle), np.cos(angle)
    high, low = split_table(table.reshape(2 * NG, 2 * NG))
    return np.concatenate([high, high, low], 0)


def table_x():
    angle = 2 * np.pi * np.arange(NG) / NG
    table = np.zeros((8, NG), np.float32)
    table[0], table[1] = np.cos(angle), np.sin(angle)
    return table


def split(x):
    high = x.astype(BF16)
    return high, (x - high.astype(F32)).astype(BF16)


def dot(a, b, contract, precision=None):
    return lax.dot_general(
        a, b, (contract, ((), ())), precision=precision, preferred_element_type=F32
    )


def kernel(
    total_pairs,
    pair_c, pair_v, energy_c, energy_v,
    psi_c, psi_v, wz, wy, wx, g_index,
    chi_real, chi_imag,
    band_v, band_c, density, z_part, y_part,
    q, core_in, chip_out, chip_in, block, z_blocks, row_blocks, col_blocks, load,
    core_send, core_recv, chip_send, chip_recv, z_send, z_recv,
    row_send, row_recv, plane_send, plane_recv, relay_send, relay_recv,
):
    f, g = lax.axis_index("fft"), lax.axis_index("grp")
    core, chip, z = f % 2, f // 2, f // 4
    x = chip % 2
    sibling = f + 1 - 2 * core

    copy_c = pltpu.make_async_copy(psi_c, band_c, load.at[0])
    copy_v = pltpu.make_async_copy(psi_v, band_v, load.at[1])
    copy_c.start()
    copy_v.start()

    def remote(src, dst, send, recv, to):
        return pltpu.make_async_remote_copy(
            src_ref=src, dst_ref=dst, send_sem=send, recv_sem=recv,
            device_id=to, device_id_type=MESH,
        )

    barrier = pltpu.get_barrier_semaphore()
    pl.semaphore_signal(barrier, 1, device_id=(sibling, g), device_id_type=MESH)

    def greet_chip(k, _):
        to = ((2 * chip + 2 * k) % 32 + core, g)
        pl.semaphore_signal(barrier, 1, device_id=to, device_id_type=MESH)
        return 0

    lax.fori_loop(1, CHIPS, greet_chip, 0)

    def greet_plane(k, _):
        to = (z * 4 + (k % 2) * 2 + core, (g + k // 2) % 8)
        pl.semaphore_signal(barrier, 1, device_id=to, device_id_type=MESH)
        return 0

    lax.fori_loop(2, 16, greet_plane, 0)

    row = lax.broadcasted_iota(jnp.int32, (BOTH, 128), 0)
    row = jnp.where(row >= PAIRS, row - PAIRS, row)

    def gaps(p, gap):
        return jnp.where(row == p, energy_c[pair_c[p]] - energy_v[pair_v[p]], gap)

    gap = lax.fori_loop(0, PAIRS, gaps, jnp.ones((BOTH, 128), F32))
    factor = jnp.sqrt(2.0 / gap) * (total_pairs ** (-0.25) * NG ** (-1.5))

    copy_v.wait()
    copy_c.wait()

    def multiply(p, _):
        start = pl.multiple_of(p * NG, NG)
        density[pl.ds(start, NG), :] = (
            band_v[pair_v[p]].astype(F32) * band_c[pair_c[p]].astype(F32)
        )
        return 0

    lax.fori_loop(0, PAIRS, multiply, 0)

    def along_z(i, _):
        lines = []
        for t in range(2):
            lines.append(jnp.concatenate(
                [density[pl.ds(4 * i + 2 * t + x, PAIRS, stride=NG), :] for x in range(2)], 0
            ))
        high, low = split(jnp.concatenate(lines, 1))
        lines = jnp.concatenate([high, low, high], 1)
        result = dot(wz[...], lines, ((1,), (1,)))
        start = pl.multiple_of(8 * i, 8)
        z_part[:, pl.ds(start, 8), 0:BOTH] = result.reshape(HALF_C, 8, BOTH)
        return 0

    lax.fori_loop(0, NG // 4, along_z, 0, unroll=8)

    lane = lax.broadcasted_iota(jnp.int32, (BOTH, 128), 1)

    def along_y(k, most):
        lines = jnp.concatenate([z_part[2 * k + c].T[0:BOTH] for c in range(2)], 0)
        high, low = split(lines)
        result = dot(jnp.concatenate([high, low, high], 1), wy[...], ((1,), (0,)))
        first, second = result[0:BOTH], result[BOTH:]
        real = jnp.where(lane < NG, first, pltpu.roll(second, NG, 1)) * factor
        imag = jnp.where(lane < NG, pltpu.roll(first, NG, 1), second) * factor
        start = pl.multiple_of(128 * k, 128)
        for i, part in enumerate(split(real) + split(imag)):
            place = (0, 2, 1, 3)[i] * BOTH
            y_part[place:place + BOTH, pl.ds(start, 128)] = part
        size = jnp.abs(real) + jnp.abs(imag)
        return jnp.maximum(most, size[0:PAIRS] + size[PAIRS:])

    most = lax.fori_loop(
        0, HALF_C // 2, along_y, jnp.zeros((PAIRS, 128), F32), unroll=HALF_C // 2
    )
    most = jnp.max(jnp.max(most, 0, keepdims=True), 1, keepdims=True)
    level = jnp.floor(jnp.log2(jnp.maximum(most, 1e-30) * 1.001)) + 1.0
    level_rows = jnp.broadcast_to(level, (8, 128))
    up = jnp.exp2(15.0 - level)

    half_lane = lax.broadcasted_iota(jnp.int32, (PAIRS, 128), 1) < NG
    key_row = lax.broadcasted_iota(jnp.int16, (KEYS, WIDE), 0)
    turn_row = lax.broadcasted_iota(jnp.int32, (NG, 2 * WIDE), 0)
    tail = lax.broadcasted_iota(jnp.int32, (128, 128), 0) >= 120

    pl.semaphore_wait(barrier, 30)

    def to_sibling(j):
        return remote(q.at[1 - core, j], core_in.at[j], core_send.at[j], core_recv.at[j], (sibling, g))

    def to_chip(j):
        return remote(
            chip_out.at[j], chip_in.at[chip], chip_send.at[j], chip_recv.at[chip], (2 * j + core, g)
        )

    def layer_of(k):
        return (z + (4 - (k + 1) // 2) * (2 * (k % 2) - 1) + 8) % 8

    def add_core(k):
        for n in range(2):
            j = 2 * layer_of(k) + n
            to_sibling(j).wait_recv()
            own = q[core, j].astype(jnp.int32).astype(F32)
            other = core_in[j].astype(jnp.int32).astype(F32)
            own_level, other_level = own[120:121], other[120:121]
            level = jnp.maximum(own_level, other_level) + 1.0
            total = own * jnp.exp2(own_level - level) + other * jnp.exp2(other_level - level)
            total = jnp.where(tail, level, jnp.floor(total + 0.5))
            chip_out[j] = total.astype(jnp.int32).astype(jnp.int16)

            @pl.when(j != chip)
            def _():
                to_chip(j).start()

    def select(k, _):
        m = layer_of(k)
        points = g_index[0:1, pl.ds(pl.multiple_of(m * WIDE, 128), WIDE)]
        a, b, c = points >> 12, (points >> 6) & 63, points & 63
        mirror = c > 32
        a = jnp.where(mirror, (NG - a) & 63, a)
        b = jnp.where(mirror, (NG - b) & 63, b)
        c = jnp.where(mirror, NG - c, c)
        key = (c * NG + b).astype(jnp.int16)
        chosen = jnp.where(key_row == key, BF16(1), BF16(0))
        picked = dot(y_part[...], chosen, ((1,), (0,)))
        picked = picked[0:2 * BOTH] + picked[2 * BOTH:]
        re0, re1, im0, im1 = (picked[i * PAIRS:(i + 1) * PAIRS] for i in range(4))
        turns = jnp.concatenate([(a * (2 * f)) & 63, (a * (2 * f + 1)) & 63], 1)
        phase = dot(wx[...], (turn_row == turns).astype(F32), ((1,), (0,)), lax.Precision.HIGHEST)
        cos0, cos1 = phase[0:1, 0:WIDE], phase[0:1, WIDE:]
        sin0, sin1 = phase[1:2, 0:WIDE], phase[1:2, WIDE:]
        sign = jnp.where(mirror, -up, up)
        real = (cos0 * re0 + sin0 * im0 + cos1 * re1 + sin1 * im1) * up
        imag = (cos0 * im0 - sin0 * re0 + cos1 * im1 - sin1 * re1) * sign
        real, imag = jnp.floor(real + 0.5), jnp.floor(imag + 0.5)
        for n in range(2):
            at = n * CHIP_POINTS
            middle_re, middle_im = real[:, at + 128:at + 256], imag[:, at + 128:at + 256]
            for side in range(2):
                if side == 0:
                    middle = jnp.where(half_lane, middle_re, pltpu.roll(middle_im, NG, 1))
                else:
                    middle = jnp.where(half_lane, pltpu.roll(middle_re, NG, 1), middle_im)
                lanes = slice(at + 256 * side, at + 256 * side + 128)
                slab = jnp.concatenate([real[:, lanes], imag[:, lanes], middle, level_rows], 0)
                q[side, 2 * m + n] = slab.astype(jnp.int32).astype(jnp.int16)
        for n in range(2):
            to_sibling(2 * m + n).start()

        @pl.when(k > 0)
        def _():
            add_core(k - 1)

        return 0

    lax.fori_loop(0, 8, select, 0)
    add_core(7)

    def scaled(slab):
        slab = slab.astype(jnp.int32).astype(F32)
        return slab * jnp.exp2(slab[120:121] - 15.0)

    def add_chip(k, total):
        j = (chip + k) % CHIPS
        remote(
            chip_out.at[j], chip_in.at[j], chip_send.at[j], chip_recv.at[j], (2 * j + core, g)
        ).wait_recv()
        return total + scaled(chip_in[j])

    total = lax.fori_loop(1, CHIPS, add_chip, scaled(chip_out[chip]))
    block[...] = jnp.where(tail, 0.0, total).astype(BF16)

    def to_z(k):
        other = (z + k) % 8
        return remote(
            block, z_blocks.at[z], z_send.at[other], z_recv.at[z], (other * 4 + x * 2 + core, g)
        )

    def to_row(k):
        other = (g + k) % 8
        return remote(block, row_blocks.at[g], row_send.at[other], row_recv.at[g], (f, other))

    def send_block(k, _):
        to_z(k).start()
        to_row(k).start()
        return 0

    lax.fori_loop(1, 8, send_block, 0)
    z_blocks[z] = block[...]
    row_blocks[g] = block[...]

    def to_plane(layer, to_x):
        return remote(
            z_blocks.at[layer], col_blocks.at[core, x, g],
            plane_send.at[layer, to_x], plane_recv.at[x, g], (z * 4 + to_x * 2 + core, layer),
        )

    def stays(layer, to_x):
        return jnp.logical_and(layer == g, to_x == x)

    def spread(k, _):
        layer = (z + (k + 1) // 2 * (1 - 2 * (k % 2)) + 8) % 8

        @pl.when(k > 0)
        def _():
            remote(
                block, z_blocks.at[layer], z_send.at[layer], z_recv.at[layer],
                (layer * 4 + x * 2 + core, g),
            ).wait_recv()

        for to_x in range(2):
            @pl.when(stays(layer, to_x))
            def _():
                col_blocks[core, x, g] = z_blocks[layer]

            @pl.when(jnp.logical_not(stays(layer, to_x)))
            def _():
                to_plane(layer, to_x).start()

        return 0

    lax.fori_loop(0, 8, spread, 0)

    def relay(side, from_x, from_g):
        return remote(
            col_blocks.at[side, from_x, from_g], col_blocks.at[side, from_x, from_g],
            relay_send.at[from_x, from_g], relay_recv.at[from_x, from_g], (sibling, g),
        )

    def pass_on(k, _):
        from_x, from_g = (x + k) % 2, (g + k // 2) % 8

        @pl.when(k > 0)
        def _():
            remote(
                z_blocks.at[0], col_blocks.at[core, from_x, from_g],
                plane_send.at[0, 0], plane_recv.at[from_x, from_g],
                (z * 4 + from_x * 2 + core, from_g),
            ).wait_recv()

        relay(core, from_x, from_g).start()
        return 0

    lax.fori_loop(0, 16, pass_on, 0)

    def row_arrives(k, _):
        other = (g + k) % 8
        remote(
            block, row_blocks.at[other], row_send.at[other], row_recv.at[other], (f, other)
        ).wait_recv()
        return 0

    lax.fori_loop(1, 8, row_arrives, 0)

    def relay_arrives(k, _):
        relay(1 - core, k % 2, k // 2).wait_recv()
        return 0

    lax.fori_loop(0, 16, relay_arrives, 0)

    half_lane = lax.broadcasted_iota(jnp.int32, (8 * PAIRS, 128), 1) < NG

    def gather(read):
        blocks = [read(i).astype(F32) for i in range(8)]
        return tuple(
            jnp.concatenate([b[s * PAIRS:(s + 1) * PAIRS] for b in blocks], 0) for s in range(3)
        )

    real, imag, middle = gather(lambda i: row_blocks[i])
    full = jnp.concatenate([real, imag], 0).astype(BF16)
    half = jnp.concatenate([middle, pltpu.roll(middle, NG, 1)], 0)[:, 0:NG].astype(BF16)
    full_row = pl.multiple_of(core * NG, NG)
    half_row = pl.multiple_of((1 - core) * 128, NG)
    for side in range(2):
        real0, imag0, middle0 = gather(lambda i: col_blocks[0, side, i])
        real2, imag2, middle2 = gather(lambda i: col_blocks[1, side, i])
        real1 = jnp.where(half_lane, middle0, pltpu.roll(middle2, NG, 1))
        imag1 = jnp.where(half_lane, pltpu.roll(middle0, NG, 1), middle2)
        real = jnp.concatenate([real0, real1, real2], 1)
        imag = jnp.concatenate([imag0, imag1, imag2], 1)
        right_sum = jnp.concatenate([real, imag], 0).astype(BF16)
        right_cross = jnp.concatenate([imag, -real], 0).astype(BF16)
        lanes = slice(side * CHIP_POINTS, (side + 1) * CHIP_POINTS)
        for left, rows in ((full, pl.ds(full_row, 128)), (half, pl.ds(half_row, NG))):
            chi_real[rows, lanes] = -dot(left, right_sum, ((0,), (0,)))
            chi_imag[rows, lanes] = dot(left, right_cross, ((0,), (0,)))

    def drain_chips(k, _):
        to_sibling((chip + k) % CHIPS).wait_send()

        @pl.when(k < CHIPS)
        def _():
            to_chip((chip + k) % CHIPS).wait_send()

        return 0

    lax.fori_loop(1, CHIPS + 1, drain_chips, 0)

    def drain_blocks(k, _):
        to_z(k).wait_send()
        to_row(k).wait_send()
        return 0

    lax.fori_loop(1, 8, drain_blocks, 0)

    def drain_plane(k, _):
        @pl.when(jnp.logical_not(stays(k // 2, k % 2)))
        def _():
            to_plane(k // 2, k % 2).wait_send()

        relay(core, k % 2, k // 2).wait_send()
        return 0

    lax.fori_loop(0, 16, drain_plane, 0)


def per_device(
    psi_valence,
    psi_conduction,
    energy_valence,
    energy_conduction,
    pair_valence,
    pair_conduction,
    g_index,
):
    def tiles(psi):
        bands = psi.shape[0]
        return psi.reshape(bands, 2, 32, 128).transpose(0, 2, 1, 3).reshape(bands, NG, 128)

    psi_c, psi_v = tiles(psi_conduction), tiles(psi_valence)
    points = g_index.shape[0]
    shape = jax.ShapeDtypeStruct(
        (points // lax.axis_size("fft"), points // lax.axis_size("grp")), F32
    )
    smem = pl.BlockSpec(memory_space=pltpu.SMEM)
    vmem = pl.BlockSpec(memory_space=pltpu.VMEM)
    anywhere = pl.BlockSpec(memory_space=pl.ANY)
    dma = pltpu.SemaphoreType.DMA
    slabs = pltpu.VMEM((CHIPS, 128, 128), jnp.int16)
    blocks = pltpu.VMEM((8, 128, 128), BF16)
    return pl.pallas_call(
        functools.partial(kernel, PAIRS * lax.axis_size("grp")),
        out_shape=(shape, shape),
        in_specs=[smem] * 4 + [anywhere] * 2 + [vmem] * 4,
        out_specs=(vmem, vmem),
        scratch_shapes=[
            pltpu.VMEM(psi_v.shape, BF16),
            pltpu.VMEM(psi_c.shape, BF16),
            pltpu.VMEM((PAIRS * NG, 128), F32),
            pltpu.VMEM((HALF_C, 128, 128), F32),
            pltpu.VMEM((4 * BOTH, KEYS), BF16),
            pltpu.VMEM((2, CHIPS, 128, 128), jnp.int16),
            slabs, slabs, slabs,
            pltpu.VMEM((128, 128), BF16),
            blocks, blocks,
            pltpu.VMEM((2, 2, 8, 128, 128), BF16),
            dma((2,)),
            dma((CHIPS,)), dma((CHIPS,)), dma((CHIPS,)), dma((CHIPS,)),
            dma((8,)), dma((8,)), dma((8,)), dma((8,)),
            dma((8, 2)), dma((2, 8)), dma((2, 8)), dma((2, 8)),
        ],
        compiler_params=pltpu.CompilerParams(
            collective_id=0, has_side_effects=True, vmem_limit_bytes=62 * 1024 * 1024
        ),
    )(
        pair_conduction, pair_valence, energy_conduction, energy_valence, psi_c, psi_v,
        jnp.asarray(table_z()), jnp.asarray(table_y()), jnp.asarray(table_x()),
        g_index.reshape(1, -1),
    )


def solution(mesh):
    placed = (P(None, "fft", None), P(None, "fft", None), P(), P(), P("grp"), P("grp"), P())
    return jax.shard_map(
        per_device,
        mesh=mesh,
        in_specs=placed,
        out_specs=(P("fft", "grp"), P("fft", "grp")),
        check_vma=False,
    )
```

```python
import functools
import math

import jax
import jax.numpy as jnp
import ml_dtypes
import numpy as np
from jax import lax
from jax.experimental import pallas as pl
from jax.experimental.pallas import tpu as pltpu
from jax.sharding import PartitionSpec as P

NG = 64
HALF_C = 34
KEYS = HALF_C * NG
PAIRS = 40
BOTH = 2 * PAIRS
CHIPS = 16
CHIP_POINTS = 384
WIDE = 512
FULL, MIDDLE = 80, 48
BF16 = jnp.bfloat16
F32 = jnp.float32
FP8 = jnp.float8_e4m3fn
MESH = pl.DeviceIdType.MESH


def split_table(table):
    high = table.astype(ml_dtypes.bfloat16)
    low = (table - high.astype(np.float64)).astype(ml_dtypes.bfloat16)
    return high, low


def table_z():
    c, z = np.arange(33)[:, None], np.arange(NG)[None, :]
    angle = 2 * np.pi * ((c * z) % NG) / NG
    table = np.zeros((HALF_C, 4, 2, 4, NG))
    for y in range(4):
        table[:33, y, 0, y] = np.cos(angle)
        table[:33, y, 1, y] = -np.sin(angle)
    high, low = split_table(table.reshape(HALF_C * 8, 4 * NG))
    return np.concatenate([high, high, low], 1)


def table_y():
    y, b = np.arange(NG)[:, None], np.arange(NG)[None, :]
    angle = 2 * np.pi * ((y * b) % NG) / NG
    table = np.zeros((NG, 2, 2, NG))
    table[:, 0, 0], table[:, 0, 1] = np.cos(angle), -np.sin(angle)
    table[:, 1, 0], table[:, 1, 1] = np.sin(angle), np.cos(angle)
    high, low = split_table(table.reshape(2 * NG, 2 * NG))
    return np.concatenate([high, high, low], 0)


def table_x():
    angle = 2 * np.pi * np.arange(NG) / NG
    table = np.zeros((8, NG), np.float32)
    table[0], table[1] = np.cos(angle), np.sin(angle)
    return table


def split(x):
    high = x.astype(BF16)
    return high, (x - high.astype(F32)).astype(BF16)


def dot(a, b, contract, precision=None):
    return lax.dot_general(
        a, b, (contract, ((), ())), precision=precision, preferred_element_type=F32
    )


def kernel(
    total_pairs,
    pair_c, pair_v, energy_c, energy_v,
    psi_c, psi_v, wz, wy, wx, g_index,
    chi_real, chi_imag,
    band_v, band_c, density, z_part, y_part, bounds, scales,
    own1, own2, core_in1, core_in2, chip_out1, chip_out2, chip_in1, chip_in2,
    block1, block2, z_blocks1, z_blocks2, row_blocks1, row_blocks2, col_blocks1, col_blocks2,
    load, bound_send, bound_recv, scale_send, scale_recv,
    core_send, core_recv, chip_send, chip_recv, z_send, z_recv,
    row_send, row_recv, plane_send, plane_recv, relay_send, relay_recv,
):
    own, core_in = (own1, own2), (core_in1, core_in2)
    chip_out, chip_in = (chip_out1, chip_out2), (chip_in1, chip_in2)
    block, z_blocks = (block1, block2), (z_blocks1, z_blocks2)
    row_blocks, col_blocks = (row_blocks1, row_blocks2), (col_blocks1, col_blocks2)
    f, g = lax.axis_index("fft"), lax.axis_index("grp")
    core, chip, z = f % 2, f // 2, f // 4
    x = chip % 2
    sibling = f + 1 - 2 * core

    copy_c = pltpu.make_async_copy(psi_c, band_c, load.at[0])
    copy_v = pltpu.make_async_copy(psi_v, band_v, load.at[1])
    copy_c.start()
    copy_v.start()

    def remote(src, dst, send, recv, to):
        return pltpu.make_async_remote_copy(
            src_ref=src, dst_ref=dst, send_sem=send, recv_sem=recv,
            device_id=to, device_id_type=MESH,
        )

    barrier = pltpu.get_barrier_semaphore()
    pl.semaphore_signal(barrier, 1, device_id=(sibling, g), device_id_type=MESH)

    def greet_chip(k, _):
        to = ((2 * chip + 2 * k) % 32 + core, g)
        pl.semaphore_signal(barrier, 1, device_id=to, device_id_type=MESH)
        return 0

    lax.fori_loop(1, CHIPS, greet_chip, 0)

    def greet_plane(k, _):
        to = (z * 4 + (k % 2) * 2 + core, (g + k // 2) % 8)
        pl.semaphore_signal(barrier, 1, device_id=to, device_id_type=MESH)
        return 0

    lax.fori_loop(2, 16, greet_plane, 0)

    column = lax.broadcasted_iota(jnp.int32, (8, BOTH), 1)
    column = jnp.where(column >= PAIRS, column - PAIRS, column)

    def gaps(p, gap):
        return jnp.where(column == p, energy_c[pair_c[p]] - energy_v[pair_v[p]], gap)

    gap = lax.fori_loop(0, PAIRS, gaps, jnp.ones((8, BOTH), F32))
    factor = jnp.sqrt(2.0 / gap) * (total_pairs ** (-0.25) * NG ** (-1.5))

    copy_v.wait()
    copy_c.wait()

    def multiply(p, _):
        start = pl.multiple_of(p * NG, NG)
        density[pl.ds(start, NG), :] = (
            band_v[pair_v[p]].astype(F32) * band_c[pair_c[p]].astype(F32)
        )
        return 0

    lax.fori_loop(0, PAIRS, multiply, 0)

    def along_z(i, size):
        lines = []
        for t in range(2):
            lines.append(jnp.concatenate([
                density[pl.ds(4 * i + 2 * t + n, PAIRS, stride=NG), :] for n in range(2)
            ], 0))
        high, low = split(jnp.concatenate(lines, 1))
        lines = jnp.concatenate([high, low, high], 1)
        result = dot(wz[...], lines, ((1,), (1,))).reshape(HALF_C, 8, BOTH) * factor
        start = pl.multiple_of(8 * i, 8)
        z_part[:, pl.ds(start, 8), 0:BOTH] = result
        return size + jnp.abs(result)

    size = lax.fori_loop(
        0, NG // 4, along_z, jnp.zeros((HALF_C, 8, BOTH), F32), unroll=8
    )
    size = jnp.max(jnp.sum(size, 1), 0, keepdims=True)
    most = jnp.maximum(jnp.max(size, 1, keepdims=True), 1e-30)
    size = jnp.max(size[:, 0:PAIRS] + size[:, PAIRS:], 1, keepdims=True)
    bounds[core] = jnp.broadcast_to(jnp.maximum(size, 1e-30), (8, 128))
    fit = 400.0 / most

    pl.semaphore_wait(barrier, 30)
    swap = remote(bounds.at[core], bounds.at[core], bound_send.at[0], bound_recv.at[0], (sibling, g))
    swap.start()

    lane = lax.broadcasted_iota(jnp.int32, (BOTH, 128), 1)

    def along_y(k, _):
        lines = jnp.concatenate([z_part[2 * k + n].T[0:BOTH] for n in range(2)], 0)
        high, low = split(lines)
        result = dot(jnp.concatenate([high, low, high], 1), wy[...], ((1,), (0,)))
        first, second = result[0:BOTH], result[BOTH:]
        real = jnp.where(lane < NG, first, pltpu.roll(second, NG, 1))
        imag = jnp.where(lane < NG, pltpu.roll(first, NG, 1), second)
        rest = jnp.concatenate([real, imag], 0) * fit
        start = pl.multiple_of(128 * k, 128)
        for i in range(3):
            piece = rest.astype(FP8)
            y_part[2 * BOTH * i:2 * BOTH * (i + 1), pl.ds(start, 128)] = piece
            rest = rest - piece.astype(F32)
        return 0

    lax.fori_loop(0, HALF_C // 2, along_y, 0, unroll=HALF_C // 2)

    swap.wait_recv()
    bound = (bounds[0] + bounds[1]) * 1.001
    scales[chip] = bound * (1.0 / 32767.0)
    up = (32767.0 / fit) / bound[0:1, 0:1]

    def to_scale(j):
        return remote(
            scales.at[chip], scales.at[chip], scale_send.at[j], scale_recv.at[chip], (2 * j + core, g)
        )

    def send_scale(k, _):
        to_scale((chip + k) % CHIPS).start()
        return 0

    lax.fori_loop(1, CHIPS, send_scale, 0)

    half_lane = lax.broadcasted_iota(jnp.int32, (PAIRS, 128), 1) < NG
    key_row = lax.broadcasted_iota(jnp.int16, (KEYS, WIDE), 0)
    turn_row = lax.broadcasted_iota(jnp.int32, (NG, 2 * WIDE), 0)

    def to_sibling(h, j):
        return remote(
            own[h].at[1 - core, j], core_in[h].at[j], core_send.at[h, j], core_recv.at[h, j], (sibling, g)
        )

    def to_chip(h, j):
        return remote(
            chip_out[h].at[j], chip_in[h].at[chip],
            chip_send.at[h, j], chip_recv.at[h, chip], (2 * j + core, g),
        )

    def layer_of(k):
        return (z + (4 - (k + 1) // 2) * (2 * (k % 2) - 1) + 8) % 8

    def chips_of(h, k):
        layers = (k,) if h == 0 else (2 * k, 2 * k + 1)
        return [2 * layer_of(i) + n for i in layers for n in range(2)]

    def add_core(h, k):
        for j in chips_of(h, k):
            total = jnp.floor(own[h][core, j] + core_in[h][j] + 0.5).astype(jnp.int32)
            if h == 1:
                total = jnp.concatenate([total, jnp.zeros((MIDDLE - PAIRS, 128), jnp.int32)], 0)
            chip_out[h][j] = total.astype(jnp.int16)

    def arrive(h, k):
        for j in chips_of(h, k):
            to_sibling(h, j).wait_recv()

    def send(h, k, last):
        for j in chips_of(h, k):
            if last:
                @pl.when(j != chip)
                def _():
                    to_chip(h, j).start()
            else:
                to_chip(h, j).start()

    def select(h, k):
        chips = chips_of(h, k)
        tiles = [(j, t) for j in chips for t in ((0, 2) if h == 0 else (1,))]
        points = jnp.concatenate([
            g_index[0:1, pl.ds(pl.multiple_of(j * CHIP_POINTS + t * 128, 128), 128)]
            for j, t in tiles
        ], 1)
        a, b, c = points >> 12, (points >> 6) & 63, points & 63
        mirror = c > 32
        a = jnp.where(mirror, (NG - a) & 63, a)
        b = jnp.where(mirror, (NG - b) & 63, b)
        c = jnp.where(mirror, NG - c, c)
        key = (c * NG + b).astype(jnp.int16)
        chosen = jnp.where(key_row == key, BF16(1), BF16(0)).astype(FP8)
        picked = dot(y_part[...], chosen, ((1,), (0,)))
        picked = picked[0:2 * BOTH] + (picked[2 * BOTH:4 * BOTH] + picked[4 * BOTH:])
        re0, re1, im0, im1 = (picked[i * PAIRS:(i + 1) * PAIRS] for i in range(4))
        turns = jnp.concatenate([(a * (2 * f)) & 63, (a * (2 * f + 1)) & 63], 1)
        phase = dot(wx[...], (turn_row == turns).astype(F32), ((1,), (0,)), lax.Precision.HIGHEST)
        phase = phase * up
        cos0, cos1 = phase[0:1, 0:WIDE], phase[0:1, WIDE:]
        sin0, sin1 = phase[1:2, 0:WIDE], phase[1:2, WIDE:]
        real = cos0 * re0 + sin0 * im0 + cos1 * re1 + sin1 * im1
        imag = cos0 * im0 - sin0 * re0 + cos1 * im1 - sin1 * re1
        imag = jnp.where(mirror, -imag, imag)
        for n, (j, t) in enumerate(tiles):
            re, im = real[:, 128 * n:128 * (n + 1)], imag[:, 128 * n:128 * (n + 1)]
            if h == 0:
                own1[t // 2, j] = jnp.concatenate([re, im], 0)
            else:
                own2[0, j] = jnp.where(half_lane, re, pltpu.roll(im, NG, 1))
                own2[1, j] = jnp.where(half_lane, pltpu.roll(re, NG, 1), im)
        return chips

    def hand_over(h, chips):
        for j in chips:
            to_sibling(h, j).start()

    def step(h, k, added=None):
        if added is not None:
            arrive(*added)
        chips = select(h, k)
        if added is not None:
            add_core(*added)
        hand_over(h, chips)
        if added is not None:
            send(*added, False)

    def loop(first, last, body):
        def run(k, _):
            body(k)
            return 0
        lax.fori_loop(first, last, run, 0)

    loop(0, 2, lambda k: step(0, k))
    loop(2, 8, lambda k: step(0, k, (0, k - 2)))
    arrive(0, 6)
    chips = select(1, 0)
    add_core(0, 6)
    hand_over(1, chips)
    send(0, 6, False)
    arrive(0, 7)
    chips = select(1, 1)
    add_core(0, 7)
    hand_over(1, chips)
    send(0, 7, True)
    loop(2, 4, lambda k: step(1, k, (1, k - 2)))
    for k in (2, 3):
        arrive(1, k)
        add_core(1, k)
        send(1, k, k == 3)

    def scale_arrives(k):
        j = (chip + k) % CHIPS
        remote(
            scales.at[j], scales.at[j], scale_send.at[j], scale_recv.at[j], (2 * j + core, g)
        ).wait_recv()

    loop(1, CHIPS, scale_arrives)

    def to_z(h, k):
        other = (z + k) % 8
        return remote(
            block[h], z_blocks[h].at[z], z_send.at[h, other], z_recv.at[h, z],
            (other * 4 + x * 2 + core, g),
        )

    def to_row(h, k):
        other = (g + k) % 8
        return remote(
            block[h], row_blocks[h].at[g], row_send.at[h, other], row_recv.at[h, g], (f, other)
        )

    def near(k):
        return (k + 1) // 2 * (1 - 2 * (k % 2)) + 8

    for h in range(2):
        chip_in[h][chip] = chip_out[h][chip]

        def add_layer(k, total):
            layer = (2 * z - layer_of(k) + 8) % 8
            for n in range(2):
                j = 2 * layer + n

                @pl.when(j != chip)
                def _():
                    remote(
                        chip_out[h].at[j], chip_in[h].at[j],
                        chip_send.at[h, j], chip_recv.at[h, j], (2 * j + core, g),
                    ).wait_recv()

                total = total + chip_in[h][j].astype(jnp.int32).astype(F32) * scales[j, 0:1]
            return total

        total = lax.fori_loop(0, 8, add_layer, jnp.zeros(block[h].shape, F32))
        block[h][...] = total.astype(BF16)
        loop(1, 8, lambda k: to_z(h, near(k)).start())
        loop(1, 8, lambda k: to_row(h, k).start())
        z_blocks[h][z] = block[h][...]
        row_blocks[h][g] = block[h][...]

    def to_plane(h, layer, to_x):
        return remote(
            z_blocks[h].at[layer], col_blocks[h].at[core, x, g],
            plane_send.at[h, layer, to_x], plane_recv.at[h, x, g],
            (z * 4 + to_x * 2 + core, layer),
        )

    def stays(layer, to_x):
        return jnp.logical_and(layer == g, to_x == x)

    for h in range(2):
        def spread(k):
            layer = (z + near(k)) % 8

            @pl.when(k > 0)
            def _():
                remote(
                    block[h], z_blocks[h].at[layer], z_send.at[h, layer], z_recv.at[h, layer],
                    (layer * 4 + x * 2 + core, g),
                ).wait_recv()

            for to_x in range(2):
                @pl.when(stays(layer, to_x))
                def _():
                    col_blocks[h][core, x, g] = z_blocks[h][layer]

                @pl.when(jnp.logical_not(stays(layer, to_x)))
                def _():
                    to_plane(h, layer, to_x).start()

        loop(0, 8, spread)

    def relay(h, side, from_x, from_g):
        return remote(
            col_blocks[h].at[side, from_x, from_g], col_blocks[h].at[side, from_x, from_g],
            relay_send.at[h, from_x, from_g], relay_recv.at[h, from_x, from_g], (sibling, g),
        )

    for h in range(2):
        def pass_on(k):
            from_x, from_g = (x + k) % 2, (g + k // 2) % 8

            @pl.when(k > 0)
            def _():
                remote(
                    z_blocks[h].at[0], col_blocks[h].at[core, from_x, from_g],
                    plane_send.at[h, 0, 0], plane_recv.at[h, from_x, from_g],
                    (z * 4 + from_x * 2 + core, from_g),
                ).wait_recv()

            relay(h, core, from_x, from_g).start()

        loop(0, 16, pass_on)

    for h in range(2):
        def row_arrives(k):
            other = (g + k) % 8
            remote(
                block[h], row_blocks[h].at[other], row_send.at[h, other], row_recv.at[h, other], (f, other)
            ).wait_recv()

        loop(1, 8, row_arrives)
        loop(0, 16, lambda k: relay(h, 1 - core, k % 2, k // 2).wait_recv())

    half_wide = lax.broadcasted_iota(jnp.int32, (8 * PAIRS, 128), 1) < NG

    def gather(read1, read2):
        blocks1 = [read1(i).astype(F32) for i in range(8)]
        blocks2 = [read2(i).astype(F32) for i in range(8)]
        return (
            jnp.concatenate([b[0:PAIRS] for b in blocks1], 0),
            jnp.concatenate([b[PAIRS:] for b in blocks1], 0),
            jnp.concatenate([b[0:PAIRS] for b in blocks2], 0),
        )

    real, imag, middle = gather(lambda i: row_blocks1[i], lambda i: row_blocks2[i])
    full = jnp.concatenate([real, imag], 0).astype(BF16)
    half = jnp.concatenate([middle, pltpu.roll(middle, NG, 1)], 0)[:, 0:NG].astype(BF16)
    full_row = pl.multiple_of(core * NG, NG)
    half_row = pl.multiple_of((1 - core) * 128, NG)
    for side in range(2):
        real0, imag0, middle0 = gather(
            lambda i: col_blocks1[0, side, i], lambda i: col_blocks2[0, side, i]
        )
        real2, imag2, middle2 = gather(
            lambda i: col_blocks1[1, side, i], lambda i: col_blocks2[1, side, i]
        )
        real1 = jnp.where(half_wide, middle0, pltpu.roll(middle2, NG, 1))
        imag1 = jnp.where(half_wide, pltpu.roll(middle0, NG, 1), middle2)
        real = jnp.concatenate([real0, real1, real2], 1)
        imag = jnp.concatenate([imag0, imag1, imag2], 1)
        right_sum = jnp.concatenate([real, imag], 0).astype(BF16)
        right_cross = jnp.concatenate([imag, -real], 0).astype(BF16)
        lanes = slice(side * CHIP_POINTS, (side + 1) * CHIP_POINTS)
        for left, rows in ((full, pl.ds(full_row, 128)), (half, pl.ds(half_row, NG))):
            chi_real[rows, lanes] = -dot(left, right_sum, ((0,), (0,)))
            chi_imag[rows, lanes] = dot(left, right_cross, ((0,), (0,)))

    swap.wait_send()

    def drain_chips(k):
        to_scale((chip + k) % CHIPS).wait_send()
        for h in range(2):
            to_chip(h, (chip + k) % CHIPS).wait_send()

    loop(1, CHIPS, drain_chips)

    def drain_blocks(k):
        for h in range(2):
            to_z(h, k).wait_send()
            to_row(h, k).wait_send()

    loop(1, 8, drain_blocks)

    def drain_plane(k):
        for h in range(2):
            to_sibling(h, k).wait_send()

            @pl.when(jnp.logical_not(stays(k // 2, k % 2)))
            def _():
                to_plane(h, k // 2, k % 2).wait_send()

            relay(h, core, k % 2, k // 2).wait_send()

    loop(0, 16, drain_plane)


def per_device(
    psi_valence,
    psi_conduction,
    energy_valence,
    energy_conduction,
    pair_valence,
    pair_conduction,
    g_index,
):
    def tiles(psi):
        bands = psi.shape[0]
        return psi.reshape(bands, 2, 32, 128).transpose(0, 2, 1, 3).reshape(bands, NG, 128)

    psi_c, psi_v = tiles(psi_conduction), tiles(psi_valence)
    points = g_index.shape[0]
    shape = jax.ShapeDtypeStruct(
        (points // lax.axis_size("fft"), points // lax.axis_size("grp")), F32
    )
    smem = pl.BlockSpec(memory_space=pltpu.SMEM)
    vmem = pl.BlockSpec(memory_space=pltpu.VMEM)
    anywhere = pl.BlockSpec(memory_space=pl.ANY)
    dma = pltpu.SemaphoreType.DMA

    def both(dtype, *lead):
        return [pltpu.VMEM((*lead, rows, 128), dtype) for rows in (FULL, MIDDLE)]

    return pl.pallas_call(
        functools.partial(kernel, PAIRS * lax.axis_size("grp")),
        out_shape=(shape, shape),
        in_specs=[smem] * 4 + [anywhere] * 2 + [vmem] * 4,
        out_specs=(vmem, vmem),
        scratch_shapes=[
            pltpu.VMEM(psi_v.shape, BF16),
            pltpu.VMEM(psi_c.shape, BF16),
            pltpu.VMEM((PAIRS * NG, 128), F32),
            pltpu.VMEM((HALF_C, 128, 128), F32),
            pltpu.VMEM((6 * BOTH, KEYS), FP8),
            pltpu.VMEM((2, 8, 128), F32),
            pltpu.VMEM((CHIPS, 8, 128), F32),
            pltpu.VMEM((2, CHIPS, FULL, 128), F32), pltpu.VMEM((2, CHIPS, PAIRS, 128), F32),
            pltpu.VMEM((CHIPS, FULL, 128), F32), pltpu.VMEM((CHIPS, PAIRS, 128), F32),
            *both(jnp.int16, CHIPS), *both(jnp.int16, CHIPS),
            *both(BF16), *both(BF16, 8), *both(BF16, 8), *both(BF16, 2, 2, 8),
            dma((2,)), dma((1,)), dma((1,)), dma((CHIPS,)), dma((CHIPS,)),
            dma((2, CHIPS)), dma((2, CHIPS)), dma((2, CHIPS)), dma((2, CHIPS)),
            dma((2, 8)), dma((2, 8)), dma((2, 8)), dma((2, 8)),
            dma((2, 8, 2)), dma((2, 2, 8)), dma((2, 2, 8)), dma((2, 2, 8)),
        ],
        compiler_params=pltpu.CompilerParams(
            collective_id=0, has_side_effects=True, vmem_limit_bytes=62 * 1024 * 1024
        ),
    )(
        pair_conduction, pair_valence, energy_conduction, energy_valence, psi_c, psi_v,
        jnp.asarray(table_z()), jnp.asarray(table_y()), jnp.asarray(table_x()),
        g_index.reshape(1, -1),
    )


def solution(mesh):
    placed = (P(None, "fft", None), P(None, "fft", None), P(), P(), P("grp"), P("grp"), P())
    return jax.shard_map(
        per_device,
        mesh=mesh,
        in_specs=placed,
        out_specs=(P("fft", "grp"), P("fft", "grp")),
        check_vma=False,
    )
```

```python
import functools
import math

import jax
import jax.numpy as jnp
import ml_dtypes
import numpy as np
from jax import lax
from jax.experimental import pallas as pl
from jax.experimental.pallas import tpu as pltpu
from jax.sharding import PartitionSpec as P

NG = 64
HALF_C = 34
KEYS = HALF_C * NG
PAIRS = 40
BOTH = 2 * PAIRS
CHIPS = 16
LOADS = 4
PIECE = NG // LOADS
CHIP_POINTS = 384
WIDE = 2 * CHIP_POINTS
BF16 = jnp.bfloat16
F32 = jnp.float32
FP8 = jnp.float8_e4m3fn
MESH = pl.DeviceIdType.MESH


def split_table(table):
    high = table.astype(ml_dtypes.bfloat16)
    low = (table - high.astype(np.float64)).astype(ml_dtypes.bfloat16)
    return high, low


def table_z():
    c, z = np.arange(33)[:, None], np.arange(NG)[None, :]
    angle = 2 * np.pi * ((c * z) % NG) / NG
    table = np.zeros((HALF_C, 4, 2, 4, NG))
    for y in range(4):
        table[:33, y, 0, y] = np.cos(angle)
        table[:33, y, 1, y] = -np.sin(angle)
    high, low = split_table(table.reshape(HALF_C * 8, 4 * NG))
    return np.concatenate([high, high, low], 1)


def table_y():
    y, b = np.arange(NG)[:, None], np.arange(NG)[None, :]
    angle = 2 * np.pi * ((y * b) % NG) / NG
    table = np.zeros((NG, 2, 2, NG))
    table[:, 0, 0], table[:, 0, 1] = np.cos(angle), -np.sin(angle)
    table[:, 1, 0], table[:, 1, 1] = np.sin(angle), np.cos(angle)
    high, low = split_table(table.reshape(2 * NG, 2 * NG))
    return np.concatenate([high, high, low], 0)


def table_x():
    angle = 2 * np.pi * np.arange(NG) / NG
    table = np.zeros((16, NG), ml_dtypes.bfloat16)
    for row, rest in ((0, np.cos(angle)), (3, np.sin(angle))):
        for i in range(3):
            table[row + i] = rest.astype(ml_dtypes.bfloat16)
            rest = rest - table[row + i].astype(np.float64)
    return table


def split(x):
    high = x.astype(BF16)
    return high, (x - high.astype(F32)).astype(BF16)


def dot(a, b, contract, precision=None):
    return lax.dot_general(
        a, b, (contract, ((), ())), precision=precision, preferred_element_type=F32
    )


def kernel(
    total_pairs,
    pair_c, pair_v, energy_c, energy_v,
    psi_c, psi_v, wz, wy, wx, g_index,
    rows_out, columns_out,
    band_v, band_c0, band_c1, band_c2, band_c3, density, z_part, y_part, point_data,
    own, core_in, chip_out, chip_in, block, z_blocks, row_blocks, col_blocks, load,
    core_send, core_recv, chip_send, chip_recv, z_send, z_recv,
    row_send, row_recv, plane_send, plane_recv, relay_send, relay_recv,
):
    f, g = lax.axis_index("fft"), lax.axis_index("grp")
    core, chip, z = f % 2, f // 2, f // 4
    x = chip % 2
    sibling = f + 1 - 2 * core
    partner = chip + 1 - 2 * x

    band_c = (band_c0, band_c1, band_c2, band_c3)

    def piece(i):
        rows = pl.ds(i * PIECE, PIECE)
        return pltpu.make_async_copy(psi_c.at[:, rows], band_c[i], load.at[8 + i])

    copy_v = pltpu.make_async_copy(psi_v, band_v, load.at[1])
    copy_v.start()
    for i in range(LOADS):
        piece(i).start()

    stores = [
        pltpu.make_async_copy(row_blocks, rows_out, load.at[2]),
        pltpu.make_async_copy(col_blocks.at[core], columns_out.at[core], load.at[3]),
        pltpu.make_async_copy(col_blocks.at[1 - core], columns_out.at[1 - core], load.at[4]),
    ]

    def remote(src, dst, send, recv, to):
        return pltpu.make_async_remote_copy(
            src_ref=src, dst_ref=dst, send_sem=send, recv_sem=recv,
            device_id=to, device_id_type=MESH,
        )

    barrier = pltpu.get_barrier_semaphore()
    pl.semaphore_signal(barrier, 1, device_id=(sibling, g), device_id_type=MESH)

    def greet_chip(k, _):
        to = ((2 * chip + 2 * k) % 32 + core, g)
        pl.semaphore_signal(barrier, 1, device_id=to, device_id_type=MESH)
        return 0

    lax.fori_loop(1, CHIPS, greet_chip, 0)

    def greet_plane(k, _):
        to = (z * 4 + (k % 2) * 2 + core, (g + k // 2) % 8)
        pl.semaphore_signal(barrier, 1, device_id=to, device_id_type=MESH)
        return 0

    lax.fori_loop(2, 16, greet_plane, 0)

    turn_row = lax.broadcasted_iota(jnp.int32, (NG, 2 * CHIP_POINTS), 0)

    def prepare(j, _):
        lanes = pl.ds(pl.multiple_of(j * CHIP_POINTS, 128), CHIP_POINTS)
        points = g_index[0:1, lanes]
        a, b, c = points >> 12, (points >> 6) & 63, points & 63
        mirror = c > 32
        a = jnp.where(mirror, (NG - a) & 63, a)
        b = jnp.where(mirror, (NG - b) & 63, b)
        c = jnp.where(mirror, NG - c, c)
        turns = jnp.concatenate([(a * (2 * f)) & 63, (a * (2 * f + 1)) & 63], 1)
        phase = dot(wx[...], jnp.where(turn_row == turns, BF16(1), BF16(0)), ((1,), (0,)))
        cos = phase[0:1] + (phase[1:2] + phase[2:3])
        sin = phase[3:4] + (phase[4:5] + phase[5:6])
        sign = jnp.where(mirror, -1.0, 1.0)
        first, second = slice(0, CHIP_POINTS), slice(CHIP_POINTS, 2 * CHIP_POINTS)
        point_data[:, lanes] = jnp.concatenate([
            cos[:, first], sin[:, first], cos[:, second], sin[:, second],
            sign, (c * NG + b).astype(F32), sign, sign,
        ], 0)
        return 0

    lax.fori_loop(0, CHIPS, prepare, 0)

    column = lax.broadcasted_iota(jnp.int32, (8, BOTH), 1)
    column = jnp.where(column >= PAIRS, column - PAIRS, column)

    def gaps(p, gap):
        return jnp.where(column == p, energy_c[pair_c[p]] - energy_v[pair_v[p]], gap)

    gap = lax.fori_loop(0, PAIRS, gaps, jnp.ones((8, BOTH), F32))
    factor = jnp.sqrt(2.0 / gap) * (total_pairs ** (-0.25) * NG ** (-1.5))

    copy_v.wait()

    def along_z(i, size):
        lines = []
        for t in range(2):
            lines.append(jnp.concatenate([
                density[pl.ds(4 * i + 2 * t + n, PAIRS, stride=NG), :] for n in range(2)
            ], 0))
        high, low = split(jnp.concatenate(lines, 1))
        lines = jnp.concatenate([high, low, high], 1)
        result = dot(wz[...], lines, ((1,), (1,))).reshape(HALF_C, 8, BOTH) * factor
        start = pl.multiple_of(8 * i, 8)
        z_part[:, pl.ds(start, 8), 0:BOTH] = result
        return size + jnp.abs(result)

    size = jnp.zeros((HALF_C, 8, BOTH), F32)
    for part in range(LOADS):
        piece(part).wait()

        def multiply(p, _):
            rows = pl.ds(part * PIECE, PIECE)
            start = pl.multiple_of(p * NG + part * PIECE, PIECE)
            density[pl.ds(start, PIECE), :] = (
                band_v[pair_v[p], rows].astype(F32) * band_c[part][pair_c[p]].astype(F32)
            )
            return 0

        lax.fori_loop(0, PAIRS, multiply, 0, unroll=4)
        for i in range(PIECE // 4):
            size = along_z(part * (PIECE // 4) + i, size)

    size = jnp.max(jnp.sum(size, 1), 0, keepdims=True)
    most = jnp.maximum(jnp.max(size, 1, keepdims=True), 1e-30)
    size = jnp.max(size[:, 0:PAIRS] + size[:, PAIRS:], 1, keepdims=True)
    bound_rows = jnp.broadcast_to(jnp.maximum(size, 1e-30), (8, 128))
    fit = 400.0 / most

    lane = lax.broadcasted_iota(jnp.int32, (BOTH, 128), 1)

    def along_y(k, _):
        lines = jnp.concatenate([z_part[2 * k + n].T[0:BOTH] for n in range(2)], 0)
        high, low = split(lines)
        result = dot(jnp.concatenate([high, low, high], 1), wy[...], ((1,), (0,)))
        first, second = result[0:BOTH], result[BOTH:]
        real = jnp.where(lane < NG, first, pltpu.roll(second, NG, 1))
        imag = jnp.where(lane < NG, pltpu.roll(first, NG, 1), second)
        rest = jnp.concatenate([real, imag], 0) * fit
        start = pl.multiple_of(128 * k, 128)
        for i in range(3):
            piece = rest.astype(FP8)
            y_part[2 * BOTH * i:2 * BOTH * (i + 1), pl.ds(start, 128)] = piece
            rest = rest - piece.astype(F32)
        return 0

    lax.fori_loop(0, HALF_C // 2, along_y, 0, unroll=HALF_C // 2)

    half_lane = lax.broadcasted_iota(jnp.int32, (PAIRS, 128), 1) < NG
    key_row = lax.broadcasted_iota(jnp.int16, (KEYS, WIDE), 0)
    tail = lax.broadcasted_iota(jnp.int32, (128, 128), 0) >= 120
    unfit = most / 400.0

    pl.semaphore_wait(barrier, 30)

    def to_sibling(j):
        return remote(
            own.at[1 - core, j], core_in.at[j], core_send.at[j], core_recv.at[j], (sibling, g)
        )

    def to_chip(j):
        return remote(
            chip_out.at[j], chip_in.at[chip], chip_send.at[j], chip_recv.at[chip], (2 * j + core, g)
        )

    def layer_of(k):
        return (z + (4 - (k + 1) // 2) * (2 * (k % 2) - 1) + 8) % 8

    def arrive(k):
        for n in range(2):
            to_sibling(2 * layer_of(k) + n).wait_recv()

    def add_core(k):
        for n in range(2):
            j = 2 * layer_of(k) + n
            total = own[core, j] + core_in[j]
            level = jnp.floor(jnp.log2(total[120:121] * 1.001)) + 1.0
            total = jnp.where(tail, level, jnp.floor(total * jnp.exp2(15.0 - level) + 0.5))
            chip_out[j] = total.astype(jnp.int32).astype(jnp.int16)

    def select(k):
        m = layer_of(k)
        data = point_data[:, pl.ds(pl.multiple_of(m * WIDE, 128), WIDE)]
        key = data[5:6].astype(jnp.int32).astype(jnp.int16)
        chosen = jnp.where(key_row == key, BF16(1), BF16(0)).astype(FP8)
        picked = dot(y_part[...], chosen, ((1,), (0,)))
        picked = picked[0:2 * BOTH] + (picked[2 * BOTH:4 * BOTH] + picked[4 * BOTH:])
        re0, re1, im0, im1 = (picked[i * PAIRS:(i + 1) * PAIRS] for i in range(4))
        turned = data * unfit
        cos0, sin0, cos1, sin1 = (turned[i:i + 1] for i in range(4))
        signed = turned * data[4:5]
        cos0_im, sin0_im, cos1_im, sin1_im = (signed[i:i + 1] for i in range(4))
        real = cos0 * re0 + sin0 * im0 + cos1 * re1 + sin1 * im1
        imag = cos0_im * im0 - sin0_im * re0 + cos1_im * im1 - sin1_im * re1
        for n in range(2):
            at = n * CHIP_POINTS
            middle_re, middle_im = real[:, at + 128:at + 256], imag[:, at + 128:at + 256]
            for side in range(2):
                if side == 0:
                    middle = jnp.where(half_lane, middle_re, pltpu.roll(middle_im, NG, 1))
                else:
                    middle = jnp.where(half_lane, pltpu.roll(middle_re, NG, 1), middle_im)
                lanes = slice(at + 256 * side, at + 256 * side + 128)
                own[side, 2 * m + n] = jnp.concatenate(
                    [real[:, lanes], imag[:, lanes], middle, bound_rows], 0
                )

    def hand_over(k):
        for n in range(2):
            to_sibling(2 * layer_of(k) + n).start()

    def send(k):
        for n in range(2):
            to_chip(2 * layer_of(k) + n).start()

    def scaled(slab):
        slab = slab.astype(jnp.int32).astype(F32)
        return slab * jnp.exp2(slab[120:121] - 15.0)

    def add_chips(k, total):
        for n in range(2):
            j = 2 * ((2 * z - layer_of(k) + 8) % 8) + n
            remote(
                chip_out.at[j], chip_in.at[j], chip_send.at[j], chip_recv.at[j], (2 * j + core, g)
            ).wait_recv()
            total = total + scaled(chip_in[j])
        return total

    def select_first(k, _):
        select(k)
        hand_over(k)
        return 0

    def select_and_add(k, _):
        select(k)
        hand_over(k)
        arrive(k - 1)
        add_core(k - 1)
        send(k - 1)
        return 0

    def select_and_sum(k, total):
        select_and_add(k, 0)
        return add_chips(k - 8, total)

    lax.fori_loop(0, 1, select_first, 0)
    lax.fori_loop(1, 8, select_and_add, 0)
    total = lax.fori_loop(8, 8, select_and_sum, jnp.zeros((128, 128), F32))
    arrive(7)
    add_core(7)
    to_chip(2 * z + 1 - x).start()
    total = lax.fori_loop(0, 7, add_chips, total + scaled(chip_out[chip]))
    remote(
        chip_out.at[partner], chip_in.at[partner], chip_send.at[partner], chip_recv.at[partner],
        (2 * partner + core, g),
    ).wait_recv()
    total = total + scaled(chip_in[partner])
    block[...] = jnp.where(tail, 0.0, total).astype(BF16)

    def to_z(k):
        other = (z + k) % 8
        return remote(
            block, z_blocks.at[z], z_send.at[other], z_recv.at[z], (other * 4 + x * 2 + core, g)
        )

    def to_row(k):
        other = (g + k) % 8
        return remote(block, row_blocks.at[g], row_send.at[other], row_recv.at[g], (f, other))

    def send_block(k, _):
        to_z(k).start()
        to_row(k).start()
        return 0

    lax.fori_loop(1, 8, send_block, 0)
    z_blocks[z] = block[...]
    row_blocks[g] = block[...]

    def to_plane(layer, to_x):
        return remote(
            z_blocks.at[layer], col_blocks.at[core, x, g],
            plane_send.at[layer, to_x], plane_recv.at[x, g], (z * 4 + to_x * 2 + core, layer),
        )

    def stays(layer, to_x):
        return jnp.logical_and(layer == g, to_x == x)

    def spread(k, _):
        layer = (z + (k + 1) // 2 * (1 - 2 * (k % 2)) + 8) % 8

        @pl.when(k > 0)
        def _():
            remote(
                block, z_blocks.at[layer], z_send.at[layer], z_recv.at[layer],
                (layer * 4 + x * 2 + core, g),
            ).wait_recv()

        for to_x in range(2):
            @pl.when(stays(layer, to_x))
            def _():
                col_blocks[core, x, g] = z_blocks[layer]

            @pl.when(jnp.logical_not(stays(layer, to_x)))
            def _():
                to_plane(layer, to_x).start()

        return 0

    lax.fori_loop(0, 8, spread, 0)

    def relay(side, from_x, from_g):
        return remote(
            col_blocks.at[side, from_x, from_g], col_blocks.at[side, from_x, from_g],
            relay_send.at[from_x, from_g], relay_recv.at[from_x, from_g], (sibling, g),
        )

    def pass_on(k, _):
        from_x, from_g = (x + k) % 2, (g + k // 2) % 8

        @pl.when(k > 0)
        def _():
            remote(
                z_blocks.at[0], col_blocks.at[core, from_x, from_g],
                plane_send.at[0, 0], plane_recv.at[from_x, from_g],
                (z * 4 + from_x * 2 + core, from_g),
            ).wait_recv()

        relay(core, from_x, from_g).start()
        return 0

    lax.fori_loop(0, 16, pass_on, 0)

    def row_arrives(k, _):
        other = (g + k) % 8
        remote(
            block, row_blocks.at[other], row_send.at[other], row_recv.at[other], (f, other)
        ).wait_recv()
        return 0

    lax.fori_loop(1, 8, row_arrives, 0)

    stores[0].start()
    stores[1].start()

    def relay_arrives(k, _):
        relay(1 - core, k % 2, k // 2).wait_recv()
        return 0

    lax.fori_loop(0, 16, relay_arrives, 0)
    stores[2].start()

    stores[0].wait()
    stores[1].wait()
    stores[2].wait()

    def drain_chips(k, _):
        to_sibling((chip + k) % CHIPS).wait_send()

        @pl.when(k < CHIPS)
        def _():
            to_chip((chip + k) % CHIPS).wait_send()

        return 0

    lax.fori_loop(1, CHIPS + 1, drain_chips, 0)

    def drain_blocks(k, _):
        to_z(k).wait_send()
        to_row(k).wait_send()
        return 0

    lax.fori_loop(1, 8, drain_blocks, 0)

    def drain_plane(k, _):
        @pl.when(jnp.logical_not(stays(k // 2, k % 2)))
        def _():
            to_plane(k // 2, k % 2).wait_send()

        relay(core, k % 2, k // 2).wait_send()
        return 0

    lax.fori_loop(0, 16, drain_plane, 0)


def product_kernel(rows_in, columns_in, chi_real, chi_imag):
    core = lax.axis_index("fft") % 2
    half_lane = lax.broadcasted_iota(jnp.int32, (8 * PAIRS, 128), 1) < NG

    def gather(read):
        blocks = [read(i).astype(F32) for i in range(8)]
        return tuple(
            jnp.concatenate([b[s * PAIRS:(s + 1) * PAIRS] for b in blocks], 0) for s in range(3)
        )

    real, imag, middle = gather(lambda i: rows_in[i])
    full = jnp.concatenate([real, imag], 0).astype(BF16)
    half = jnp.concatenate([middle, pltpu.roll(middle, NG, 1)], 0)[:, 0:NG].astype(BF16)
    full_row = pl.multiple_of(core * NG, NG)
    half_row = pl.multiple_of((1 - core) * 128, NG)
    real0, imag0, middle0 = gather(lambda i: columns_in[0, 0, i])
    real2, imag2, middle2 = gather(lambda i: columns_in[1, 0, i])
    real1 = jnp.where(half_lane, middle0, pltpu.roll(middle2, NG, 1))
    imag1 = jnp.where(half_lane, pltpu.roll(middle0, NG, 1), middle2)
    real = jnp.concatenate([real0, real1, real2], 1)
    imag = jnp.concatenate([imag0, imag1, imag2], 1)
    right_sum = jnp.concatenate([real, imag], 0).astype(BF16)
    right_cross = jnp.concatenate([imag, -real], 0).astype(BF16)
    for left, rows in ((full, pl.ds(full_row, 128)), (half, pl.ds(half_row, NG))):
        chi_real[rows, :] = -dot(left, right_sum, ((0,), (0,)))
        chi_imag[rows, :] = dot(left, right_cross, ((0,), (0,)))


def product(rows, columns, shape):
    count, width = shape.shape
    out = pl.BlockSpec((count, CHIP_POINTS), lambda side: (0, side))
    return pl.pallas_call(
        product_kernel,
        grid=(width // CHIP_POINTS,),
        out_shape=(shape, shape),
        in_specs=[
            pl.BlockSpec((8, 128, 128), lambda side: (0, 0, 0)),
            pl.BlockSpec((2, 1, 8, 128, 128), lambda side: (0, side, 0, 0, 0)),
        ],
        out_specs=(out, out),
        compiler_params=pltpu.CompilerParams(vmem_limit_bytes=56 * 1024 * 1024),
    )(rows, columns)


def per_device(
    psi_valence,
    psi_conduction,
    energy_valence,
    energy_conduction,
    pair_valence,
    pair_conduction,
    g_index,
):
    def tiles(psi):
        bands = psi.shape[0]
        return psi.reshape(bands, 2, 32, 128).transpose(0, 2, 1, 3).reshape(bands, NG, 128)

    psi_c, psi_v = tiles(psi_conduction), tiles(psi_valence)
    points = g_index.shape[0]
    shape = jax.ShapeDtypeStruct(
        (points // lax.axis_size("fft"), points // lax.axis_size("grp")), F32
    )
    smem = pl.BlockSpec(memory_space=pltpu.SMEM)
    vmem = pl.BlockSpec(memory_space=pltpu.VMEM)
    anywhere = pl.BlockSpec(memory_space=pl.ANY)
    dma = pltpu.SemaphoreType.DMA

    slabs = pltpu.VMEM((CHIPS, 128, 128), jnp.int16)
    blocks = pltpu.VMEM((8, 128, 128), BF16)
    rows, columns = pl.pallas_call(
        functools.partial(kernel, PAIRS * lax.axis_size("grp")),
        out_shape=(
            jax.ShapeDtypeStruct((8, 128, 128), BF16),
            jax.ShapeDtypeStruct((2, 2, 8, 128, 128), BF16),
        ),
        in_specs=[smem] * 4 + [anywhere] * 2 + [vmem] * 4,
        out_specs=(anywhere, anywhere),
        scratch_shapes=[
            pltpu.VMEM(psi_v.shape, BF16),
            *[pltpu.VMEM((psi_c.shape[0], PIECE, 128), BF16)] * LOADS,
            pltpu.VMEM((PAIRS * NG, 128), F32),
            pltpu.VMEM((HALF_C, 128, 128), F32),
            pltpu.VMEM((6 * BOTH, KEYS), FP8),
            pltpu.VMEM((8, points), F32),
            pltpu.VMEM((2, CHIPS, 128, 128), F32),
            pltpu.VMEM((CHIPS, 128, 128), F32),
            slabs, slabs,
            pltpu.VMEM((128, 128), BF16),
            blocks, blocks,
            pltpu.VMEM((2, 2, 8, 128, 128), BF16),
            dma((8 + LOADS,)),
            dma((CHIPS,)), dma((CHIPS,)), dma((CHIPS,)), dma((CHIPS,)),
            dma((8,)), dma((8,)), dma((8,)), dma((8,)),
            dma((8, 2)), dma((2, 8)), dma((2, 8)), dma((2, 8)),
        ],
        compiler_params=pltpu.CompilerParams(
            collective_id=0, has_side_effects=True, vmem_limit_bytes=62 * 1024 * 1024
        ),
    )(
        pair_conduction, pair_valence, energy_conduction, energy_valence, psi_c, psi_v,
        jnp.asarray(table_z()), jnp.asarray(table_y()), jnp.asarray(table_x()),
        g_index.reshape(1, -1),
    )
    return product(rows, columns, shape)


def solution(mesh):
    placed = (P(None, "fft", None), P(None, "fft", None), P(), P(), P("grp"), P("grp"), P())
    return jax.shard_map(
        per_device,
        mesh=mesh,
        in_specs=placed,
        out_specs=(P("fft", "grp"), P("fft", "grp")),
        check_vma=False,
    )
```

```python
import functools
import math

import jax
import jax.numpy as jnp
import ml_dtypes
import numpy as np
from jax import lax
from jax.experimental import pallas as pl
from jax.experimental.pallas import tpu as pltpu
from jax.sharding import PartitionSpec as P

NG = 64
HALF_C = 34
KEYS = HALF_C * NG
PAIRS = 40
BOTH = 2 * PAIRS
CHIPS = 16
JOIN_LAG = 3
LOADS = 4
PIECE = NG // LOADS
CHIP_POINTS = 384
WIDE = 2 * CHIP_POINTS
BF16 = jnp.bfloat16
F32 = jnp.float32
FP8 = jnp.float8_e4m3fn
MESH = pl.DeviceIdType.MESH


def split_table(table):
    high = table.astype(ml_dtypes.bfloat16)
    low = (table - high.astype(np.float64)).astype(ml_dtypes.bfloat16)
    return high, low


def table_z():
    c, z = np.arange(33)[:, None], np.arange(NG)[None, :]
    angle = 2 * np.pi * ((c * z) % NG) / NG
    table = np.zeros((HALF_C, 4, 2, 4, NG))
    for y in range(4):
        table[:33, y, 0, y] = np.cos(angle)
        table[:33, y, 1, y] = -np.sin(angle)
    high, low = split_table(table.reshape(HALF_C * 8, 4 * NG))
    return np.concatenate([high, high, low], 1)


def table_y():
    y, b = np.arange(NG)[:, None], np.arange(NG)[None, :]
    angle = 2 * np.pi * ((y * b) % NG) / NG
    table = np.zeros((NG, 2, 2, NG))
    table[:, 0, 0], table[:, 0, 1] = np.cos(angle), -np.sin(angle)
    table[:, 1, 0], table[:, 1, 1] = np.sin(angle), np.cos(angle)
    high, low = split_table(table.reshape(2 * NG, 2 * NG))
    return np.concatenate([high, high, low], 0)


def table_x():
    angle = 2 * np.pi * np.arange(NG) / NG
    table = np.zeros((16, NG), ml_dtypes.bfloat16)
    for row, rest in ((0, np.cos(angle)), (3, np.sin(angle))):
        for i in range(3):
            table[row + i] = rest.astype(ml_dtypes.bfloat16)
            rest = rest - table[row + i].astype(np.float64)
    return table


def split(x):
    high = x.astype(BF16)
    return high, (x - high.astype(F32)).astype(BF16)


def dot(a, b, contract, precision=None):
    return lax.dot_general(
        a, b, (contract, ((), ())), precision=precision, preferred_element_type=F32
    )


def kernel(
    total_pairs,
    pair_c, pair_v, energy_c, energy_v,
    psi_c, psi_v, wz, wy, wx, g_index,
    rows_out, columns_out,
    band_v, band_c0, band_c1, band_c2, band_c3, density, z_part, y_part, point_data,
    own, core_in, sums, x_out, x_in, chip_out, chip_in, block, z_blocks, row_blocks, col_blocks, load,
    x_send, x_recv, core_send, core_recv, chip_send, chip_recv, z_send, z_recv,
    row_send, row_recv, plane_send, plane_recv, relay_send, relay_recv,
):
    f, g = lax.axis_index("fft"), lax.axis_index("grp")
    core, chip, z = f % 2, f // 2, f // 4
    x = chip % 2
    sibling = f + 1 - 2 * core
    partner = chip + 1 - 2 * x

    band_c = (band_c0, band_c1, band_c2, band_c3)

    def piece(i):
        rows = pl.ds(i * PIECE, PIECE)
        return pltpu.make_async_copy(psi_c.at[:, rows], band_c[i], load.at[8 + i])

    copy_v = pltpu.make_async_copy(psi_v, band_v, load.at[1])
    copy_v.start()
    for i in range(LOADS):
        piece(i).start()

    stores = [
        pltpu.make_async_copy(row_blocks, rows_out, load.at[2]),
        pltpu.make_async_copy(col_blocks.at[core], columns_out.at[core], load.at[3]),
        pltpu.make_async_copy(col_blocks.at[1 - core], columns_out.at[1 - core], load.at[4]),
    ]

    def remote(src, dst, send, recv, to):
        return pltpu.make_async_remote_copy(
            src_ref=src, dst_ref=dst, send_sem=send, recv_sem=recv,
            device_id=to, device_id_type=MESH,
        )

    barrier = pltpu.get_barrier_semaphore()
    pl.semaphore_signal(barrier, 1, device_id=(sibling, g), device_id_type=MESH)

    def greet_chip(k, _):
        to = ((2 * chip + 2 * k) % 32 + core, g)
        pl.semaphore_signal(barrier, 1, device_id=to, device_id_type=MESH)
        return 0

    lax.fori_loop(1, CHIPS, greet_chip, 0)

    def greet_plane(k, _):
        to = (z * 4 + (k % 2) * 2 + core, (g + k // 2) % 8)
        pl.semaphore_signal(barrier, 1, device_id=to, device_id_type=MESH)
        return 0

    lax.fori_loop(2, 16, greet_plane, 0)

    turn_row = lax.broadcasted_iota(jnp.int32, (NG, 2 * CHIP_POINTS), 0)

    def prepare(j, _):
        lanes = pl.ds(pl.multiple_of(j * CHIP_POINTS, 128), CHIP_POINTS)
        points = g_index[0:1, lanes]
        a, b, c = points >> 12, (points >> 6) & 63, points & 63
        mirror = c > 32
        a = jnp.where(mirror, (NG - a) & 63, a)
        b = jnp.where(mirror, (NG - b) & 63, b)
        c = jnp.where(mirror, NG - c, c)
        turns = jnp.concatenate([(a * (2 * f)) & 63, (a * (2 * f + 1)) & 63], 1)
        phase = dot(wx[...], jnp.where(turn_row == turns, BF16(1), BF16(0)), ((1,), (0,)))
        cos = phase[0:1] + (phase[1:2] + phase[2:3])
        sin = phase[3:4] + (phase[4:5] + phase[5:6])
        sign = jnp.where(mirror, -1.0, 1.0)
        first, second = slice(0, CHIP_POINTS), slice(CHIP_POINTS, 2 * CHIP_POINTS)
        point_data[:, lanes] = jnp.concatenate([
            cos[:, first], sin[:, first], cos[:, second], sin[:, second],
            sign, (c * NG + b).astype(F32), sign, sign,
        ], 0)
        return 0

    lax.fori_loop(0, CHIPS, prepare, 0)

    column = lax.broadcasted_iota(jnp.int32, (8, BOTH), 1)
    column = jnp.where(column >= PAIRS, column - PAIRS, column)

    def gaps(p, gap):
        return jnp.where(column == p, energy_c[pair_c[p]] - energy_v[pair_v[p]], gap)

    gap = lax.fori_loop(0, PAIRS, gaps, jnp.ones((8, BOTH), F32))
    factor = jnp.sqrt(2.0 / gap) * (total_pairs ** (-0.25) * NG ** (-1.5))

    copy_v.wait()

    def along_z(i, size):
        lines = []
        for t in range(2):
            lines.append(jnp.concatenate([
                density[pl.ds(4 * i + 2 * t + n, PAIRS, stride=NG), :] for n in range(2)
            ], 0))
        high, low = split(jnp.concatenate(lines, 1))
        lines = jnp.concatenate([high, low, high], 1)
        result = dot(wz[...], lines, ((1,), (1,))).reshape(HALF_C, 8, BOTH) * factor
        start = pl.multiple_of(8 * i, 8)
        z_part[:, pl.ds(start, 8), 0:BOTH] = result
        return size + jnp.abs(result)

    size = jnp.zeros((HALF_C, 8, BOTH), F32)
    for part in range(LOADS):
        piece(part).wait()

        def multiply(p, _):
            rows = pl.ds(part * PIECE, PIECE)
            start = pl.multiple_of(p * NG + part * PIECE, PIECE)
            density[pl.ds(start, PIECE), :] = (
                band_v[pair_v[p], rows].astype(F32) * band_c[part][pair_c[p]].astype(F32)
            )
            return 0

        lax.fori_loop(0, PAIRS, multiply, 0, unroll=4)
        for i in range(PIECE // 4):
            size = along_z(part * (PIECE // 4) + i, size)

    size = jnp.max(jnp.sum(size, 1), 0, keepdims=True)
    most = jnp.maximum(jnp.max(size, 1, keepdims=True), 1e-30)
    size = jnp.max(size[:, 0:PAIRS] + size[:, PAIRS:], 1, keepdims=True)
    bound_rows = jnp.broadcast_to(jnp.maximum(size, 1e-30), (8, 128))
    fit = 400.0 / most

    lane = lax.broadcasted_iota(jnp.int32, (BOTH, 128), 1)

    def along_y(k, _):
        lines = jnp.concatenate([z_part[2 * k + n].T[0:BOTH] for n in range(2)], 0)
        high, low = split(lines)
        result = dot(jnp.concatenate([high, low, high], 1), wy[...], ((1,), (0,)))
        first, second = result[0:BOTH], result[BOTH:]
        real = jnp.where(lane < NG, first, pltpu.roll(second, NG, 1))
        imag = jnp.where(lane < NG, pltpu.roll(first, NG, 1), second)
        rest = jnp.concatenate([real, imag], 0) * fit
        start = pl.multiple_of(128 * k, 128)
        for i in range(3):
            piece = rest.astype(FP8)
            y_part[2 * BOTH * i:2 * BOTH * (i + 1), pl.ds(start, 128)] = piece
            rest = rest - piece.astype(F32)
        return 0

    lax.fori_loop(0, HALF_C // 2, along_y, 0, unroll=HALF_C // 2)

    half_lane = lax.broadcasted_iota(jnp.int32, (PAIRS, 128), 1) < NG
    key_row = lax.broadcasted_iota(jnp.int16, (KEYS, WIDE), 0)
    tail = lax.broadcasted_iota(jnp.int32, (128, 128), 0) >= 120
    unfit = most / 400.0

    pl.semaphore_wait(barrier, 30)

    def to_sibling(j):
        return remote(
            own.at[1 - core, j], core_in.at[j], core_send.at[j], core_recv.at[j], (sibling, g)
        )

    def to_chip(j):
        return remote(
            chip_out.at[j], chip_in.at[chip], chip_send.at[j], chip_recv.at[chip], (2 * j + core, g)
        )

    def layer_of(k):
        return (z + (4 - (k + 1) // 2) * (2 * (k % 2) - 1) + 8) % 8

    def arrive(k):
        for n in range(2):
            to_sibling(2 * layer_of(k) + n).wait_recv()

    def rounded(total, bound):
        level = jnp.floor(jnp.log2(bound * 1.001)) + 1.0
        total = jnp.where(tail, level, jnp.floor(total * jnp.exp2(15.0 - level) + 0.5))
        return total.astype(jnp.int32).astype(jnp.int16)

    def add_core(k):
        for n in range(2):
            j = 2 * layer_of(k) + n
            total = own[core, j] + core_in[j]
            chip_out[j] = rounded(total, total[120:121])

    def to_partner(m):
        return remote(
            x_out.at[m], x_in.at[m], x_send.at[m], x_recv.at[m], (2 * partner + core, g)
        )

    def add_far(k):
        m = layer_of(k)
        mine, other = 2 * m + x, 2 * m + 1 - x
        total = own[core, other] + core_in[other]
        x_out[m] = rounded(total, total[120:121])
        to_partner(m).start()
        sums[m] = own[core, mine] + core_in[mine]

    def join(k):
        m = layer_of(k)
        to_partner(m).wait_recv()
        theirs = x_in[m].astype(jnp.int32).astype(F32)
        theirs_level = theirs[120:121]
        total = sums[m] + theirs * jnp.exp2(theirs_level - 15.0)
        bound = sums[m, 120:121] + jnp.exp2(theirs_level)
        chip_out[2 * m + x] = rounded(total, bound)
        to_chip(2 * m + x).start()

    def select(k):
        m = layer_of(k)
        data = point_data[:, pl.ds(pl.multiple_of(m * WIDE, 128), WIDE)]
        key = data[5:6].astype(jnp.int32).astype(jnp.int16)
        chosen = jnp.where(key_row == key, BF16(1), BF16(0)).astype(FP8)
        picked = dot(y_part[...], chosen, ((1,), (0,)))
        picked = picked[0:2 * BOTH] + (picked[2 * BOTH:4 * BOTH] + picked[4 * BOTH:])
        re0, re1, im0, im1 = (picked[i * PAIRS:(i + 1) * PAIRS] for i in range(4))
        turned = data * unfit
        cos0, sin0, cos1, sin1 = (turned[i:i + 1] for i in range(4))
        signed = turned * data[4:5]
        cos0_im, sin0_im, cos1_im, sin1_im = (signed[i:i + 1] for i in range(4))
        real = cos0 * re0 + sin0 * im0 + cos1 * re1 + sin1 * im1
        imag = cos0_im * im0 - sin0_im * re0 + cos1_im * im1 - sin1_im * re1
        for n in range(2):
            at = n * CHIP_POINTS
            middle_re, middle_im = real[:, at + 128:at + 256], imag[:, at + 128:at + 256]
            for side in range(2):
                if side == 0:
                    middle = jnp.where(half_lane, middle_re, pltpu.roll(middle_im, NG, 1))
                else:
                    middle = jnp.where(half_lane, pltpu.roll(middle_re, NG, 1), middle_im)
                lanes = slice(at + 256 * side, at + 256 * side + 128)
                own[side, 2 * m + n] = jnp.concatenate(
                    [real[:, lanes], imag[:, lanes], middle, bound_rows], 0
                )

    def hand_over(k):
        for n in range(2):
            to_sibling(2 * layer_of(k) + n).start()

    def send(k):
        for n in range(2):
            to_chip(2 * layer_of(k) + n).start()

    def scaled(slab):
        slab = slab.astype(jnp.int32).astype(F32)
        return slab * jnp.exp2(slab[120:121] - 15.0)

    def chip_arrives(j, total):
        remote(
            chip_out.at[j], chip_in.at[j], chip_send.at[j], chip_recv.at[j], (2 * j + core, g)
        ).wait_recv()
        return total + scaled(chip_in[j])

    def add_chips(k, total):
        layer = (2 * z - layer_of(k) + 8) % 8
        return chip_arrives(2 * layer + 1, chip_arrives(2 * layer, total))

    def add_joined(k, total):
        return chip_arrives(2 * ((2 * z - layer_of(k) + 8) % 8) + x, total)

    def loop(first, last, body):
        def run(k, _):
            body(k)
            return 0

        lax.fori_loop(first, last, run, 0)

    def step(k, far, joins):
        select(k)
        hand_over(k)
        arrive(k - 1)
        if far:
            add_far(k - 1)
        else:
            add_core(k - 1)
            send(k - 1)
        if joins:
            join(k - JOIN_LAG)

    select(0)
    hand_over(0)
    step(1, False, False)
    loop(2, 1 + JOIN_LAG, lambda k: step(k, True, False))
    loop(1 + JOIN_LAG, 6, lambda k: step(k, True, True))
    loop(6, 8, lambda k: step(k, False, True))
    arrive(7)
    add_core(7)
    to_chip(2 * z + 1 - x).start()
    loop(8 - JOIN_LAG, 5, join)
    total = add_chips(0, scaled(chip_out[chip]))
    total = lax.fori_loop(1, 5, add_joined, total)
    total = lax.fori_loop(5, 7, add_chips, total)
    total = chip_arrives(partner, total)
    block[...] = jnp.where(tail, 0.0, total).astype(BF16)

    def to_z(k):
        other = (z + k) % 8
        return remote(
            block, z_blocks.at[z], z_send.at[other], z_recv.at[z], (other * 4 + x * 2 + core, g)
        )

    def to_row(k):
        other = (g + k) % 8
        return remote(block, row_blocks.at[g], row_send.at[other], row_recv.at[g], (f, other))

    def near(k):
        return (k + 1) // 2 * (1 - 2 * (k % 2)) + 8

    def send_z(k, _):
        to_z(near(k)).start()
        return 0

    def send_row(k, _):
        to_row(k).start()
        return 0

    lax.fori_loop(1, 8, send_z, 0)
    lax.fori_loop(1, 8, send_row, 0)
    z_blocks[z] = block[...]
    row_blocks[g] = block[...]

    def to_plane(layer, to_x):
        return remote(
            z_blocks.at[layer], col_blocks.at[core, x, g],
            plane_send.at[layer, to_x], plane_recv.at[x, g], (z * 4 + to_x * 2 + core, layer),
        )

    def stays(layer, to_x):
        return jnp.logical_and(layer == g, to_x == x)

    def spread(k, _):
        layer = (z + near(k)) % 8

        @pl.when(k > 0)
        def _():
            remote(
                block, z_blocks.at[layer], z_send.at[layer], z_recv.at[layer],
                (layer * 4 + x * 2 + core, g),
            ).wait_recv()

        for to_x in range(2):
            @pl.when(stays(layer, to_x))
            def _():
                col_blocks[core, x, g] = z_blocks[layer]

            @pl.when(jnp.logical_not(stays(layer, to_x)))
            def _():
                to_plane(layer, to_x).start()

        return 0

    lax.fori_loop(0, 8, spread, 0)

    def relay(side, from_x, from_g):
        return remote(
            col_blocks.at[side, from_x, from_g], col_blocks.at[side, from_x, from_g],
            relay_send.at[from_x, from_g], relay_recv.at[from_x, from_g], (sibling, g),
        )

    def pass_on(k, _):
        from_x, from_g = (x + k) % 2, (g + k // 2) % 8

        @pl.when(k > 0)
        def _():
            remote(
                z_blocks.at[0], col_blocks.at[core, from_x, from_g],
                plane_send.at[0, 0], plane_recv.at[from_x, from_g],
                (z * 4 + from_x * 2 + core, from_g),
            ).wait_recv()

        relay(core, from_x, from_g).start()
        return 0

    lax.fori_loop(0, 16, pass_on, 0)

    def row_arrives(k, _):
        other = (g + k) % 8
        remote(
            block, row_blocks.at[other], row_send.at[other], row_recv.at[other], (f, other)
        ).wait_recv()
        return 0

    lax.fori_loop(1, 8, row_arrives, 0)

    stores[0].start()
    stores[1].start()

    def relay_arrives(k, _):
        relay(1 - core, k % 2, k // 2).wait_recv()
        return 0

    lax.fori_loop(0, 16, relay_arrives, 0)
    stores[2].start()

    stores[0].wait()
    stores[1].wait()
    stores[2].wait()

    loop(0, CHIPS, lambda j: to_sibling(j).wait_send())
    for k in (0, 5, 6):
        for n in range(2):
            to_chip(2 * layer_of(k) + n).wait_send()
    for k in range(1, 5):
        to_partner(layer_of(k)).wait_send()
        to_chip(2 * layer_of(k) + x).wait_send()
    to_chip(2 * z + 1 - x).wait_send()

    def drain_blocks(k, _):
        to_z(k).wait_send()
        to_row(k).wait_send()
        return 0

    lax.fori_loop(1, 8, drain_blocks, 0)

    def drain_plane(k, _):
        @pl.when(jnp.logical_not(stays(k // 2, k % 2)))
        def _():
            to_plane(k // 2, k % 2).wait_send()

        relay(core, k % 2, k // 2).wait_send()
        return 0

    lax.fori_loop(0, 16, drain_plane, 0)


def product_kernel(rows_in, columns_in, chi_real, chi_imag):
    core = lax.axis_index("fft") % 2
    half_lane = lax.broadcasted_iota(jnp.int32, (8 * PAIRS, 128), 1) < NG

    def gather(read):
        blocks = [read(i).astype(F32) for i in range(8)]
        return tuple(
            jnp.concatenate([b[s * PAIRS:(s + 1) * PAIRS] for b in blocks], 0) for s in range(3)
        )

    real, imag, middle = gather(lambda i: rows_in[i])
    full = jnp.concatenate([real, imag], 0).astype(BF16)
    half = jnp.concatenate([middle, pltpu.roll(middle, NG, 1)], 0)[:, 0:NG].astype(BF16)
    full_row = pl.multiple_of(core * NG, NG)
    half_row = pl.multiple_of((1 - core) * 128, NG)
    real0, imag0, middle0 = gather(lambda i: columns_in[0, 0, i])
    real2, imag2, middle2 = gather(lambda i: columns_in[1, 0, i])
    real1 = jnp.where(half_lane, middle0, pltpu.roll(middle2, NG, 1))
    imag1 = jnp.where(half_lane, pltpu.roll(middle0, NG, 1), middle2)
    real = jnp.concatenate([real0, real1, real2], 1)
    imag = jnp.concatenate([imag0, imag1, imag2], 1)
    right_sum = jnp.concatenate([real, imag], 0).astype(BF16)
    right_cross = jnp.concatenate([imag, -real], 0).astype(BF16)
    for left, rows in ((full, pl.ds(full_row, 128)), (half, pl.ds(half_row, NG))):
        chi_real[rows, :] = -dot(left, right_sum, ((0,), (0,)))
        chi_imag[rows, :] = dot(left, right_cross, ((0,), (0,)))


def product(rows, columns, shape):
    count, width = shape.shape
    out = pl.BlockSpec((count, CHIP_POINTS), lambda side: (0, side))
    return pl.pallas_call(
        product_kernel,
        grid=(width // CHIP_POINTS,),
        out_shape=(shape, shape),
        in_specs=[
            pl.BlockSpec((8, 128, 128), lambda side: (0, 0, 0)),
            pl.BlockSpec((2, 1, 8, 128, 128), lambda side: (0, side, 0, 0, 0)),
        ],
        out_specs=(out, out),
        compiler_params=pltpu.CompilerParams(vmem_limit_bytes=56 * 1024 * 1024),
    )(rows, columns)


def per_device(
    psi_valence,
    psi_conduction,
    energy_valence,
    energy_conduction,
    pair_valence,
    pair_conduction,
    g_index,
):
    def tiles(psi):
        bands = psi.shape[0]
        return psi.reshape(bands, 2, 32, 128).transpose(0, 2, 1, 3).reshape(bands, NG, 128)

    psi_c, psi_v = tiles(psi_conduction), tiles(psi_valence)
    points = g_index.shape[0]
    shape = jax.ShapeDtypeStruct(
        (points // lax.axis_size("fft"), points // lax.axis_size("grp")), F32
    )
    smem = pl.BlockSpec(memory_space=pltpu.SMEM)
    vmem = pl.BlockSpec(memory_space=pltpu.VMEM)
    anywhere = pl.BlockSpec(memory_space=pl.ANY)
    dma = pltpu.SemaphoreType.DMA

    slabs = pltpu.VMEM((CHIPS, 128, 128), jnp.int16)
    blocks = pltpu.VMEM((8, 128, 128), BF16)
    rows, columns = pl.pallas_call(
        functools.partial(kernel, PAIRS * lax.axis_size("grp")),
        out_shape=(
            jax.ShapeDtypeStruct((8, 128, 128), BF16),
            jax.ShapeDtypeStruct((2, 2, 8, 128, 128), BF16),
        ),
        in_specs=[smem] * 4 + [anywhere] * 2 + [vmem] * 4,
        out_specs=(anywhere, anywhere),
        scratch_shapes=[
            pltpu.VMEM(psi_v.shape, BF16),
            *[pltpu.VMEM((psi_c.shape[0], PIECE, 128), BF16)] * LOADS,
            pltpu.VMEM((PAIRS * NG, 128), F32),
            pltpu.VMEM((HALF_C, 128, 128), F32),
            pltpu.VMEM((6 * BOTH, KEYS), FP8),
            pltpu.VMEM((8, points), F32),
            pltpu.VMEM((2, CHIPS, 128, 128), F32),
            pltpu.VMEM((CHIPS, 128, 128), F32),
            pltpu.VMEM((8, 128, 128), F32),
            pltpu.VMEM((8, 128, 128), jnp.int16), pltpu.VMEM((8, 128, 128), jnp.int16),
            slabs, slabs,
            pltpu.VMEM((128, 128), BF16),
            blocks, blocks,
            pltpu.VMEM((2, 2, 8, 128, 128), BF16),
            dma((8 + LOADS,)),
            dma((8,)), dma((8,)),
            dma((CHIPS,)), dma((CHIPS,)), dma((CHIPS,)), dma((CHIPS,)),
            dma((8,)), dma((8,)), dma((8,)), dma((8,)),
            dma((8, 2)), dma((2, 8)), dma((2, 8)), dma((2, 8)),
        ],
        compiler_params=pltpu.CompilerParams(
            collective_id=0, has_side_effects=True, vmem_limit_bytes=62 * 1024 * 1024
        ),
    )(
        pair_conduction, pair_valence, energy_conduction, energy_valence, psi_c, psi_v,
        jnp.asarray(table_z()), jnp.asarray(table_y()), jnp.asarray(table_x()),
        g_index.reshape(1, -1),
    )
    return product(rows, columns, shape)


def solution(mesh):
    placed = (P(None, "fft", None), P(None, "fft", None), P(), P(), P("grp"), P("grp"), P())
    return jax.shard_map(
        per_device,
        mesh=mesh,
        in_specs=placed,
        out_specs=(P("fft", "grp"), P("fft", "grp")),
        check_vma=False,
    )
```

```python
import functools
import math

import jax
import jax.numpy as jnp
import ml_dtypes
import numpy as np
from jax import lax
from jax.experimental import pallas as pl
from jax.experimental.pallas import tpu as pltpu
from jax.sharding import PartitionSpec as P

NG = 64
HALF_C = 34
KEYS = HALF_C * NG
PAIRS = 40
BOTH = 2 * PAIRS
CHIPS = 16
JOIN_LAG = 3
LOADS = 4
PIECE = NG // LOADS
CHIP_POINTS = 384
WIDE = 2 * CHIP_POINTS
BF16 = jnp.bfloat16
F32 = jnp.float32
FP8 = jnp.float8_e4m3fn
MESH = pl.DeviceIdType.MESH


def split_table(table):
    high = table.astype(ml_dtypes.bfloat16)
    low = (table - high.astype(np.float64)).astype(ml_dtypes.bfloat16)
    return high, low


def table_z():
    c, z = np.arange(33)[:, None], np.arange(NG)[None, :]
    angle = 2 * np.pi * ((c * z) % NG) / NG
    table = np.zeros((HALF_C, 4, 2, 4, NG))
    for y in range(4):
        table[:33, y, 0, y] = np.cos(angle)
        table[:33, y, 1, y] = -np.sin(angle)
    high, low = split_table(table.reshape(HALF_C * 8, 4 * NG))
    return np.concatenate([high, high, low], 1)


def table_y():
    y, b = np.arange(NG)[:, None], np.arange(NG)[None, :]
    angle = 2 * np.pi * ((y * b) % NG) / NG
    table = np.zeros((NG, 2, 2, NG))
    table[:, 0, 0], table[:, 0, 1] = np.cos(angle), -np.sin(angle)
    table[:, 1, 0], table[:, 1, 1] = np.sin(angle), np.cos(angle)
    high, low = split_table(table.reshape(2 * NG, 2 * NG))
    return np.concatenate([high, high, low], 0)


def table_x():
    angle = 2 * np.pi * np.arange(NG) / NG
    table = np.zeros((16, NG), ml_dtypes.bfloat16)
    for row, rest in ((0, np.cos(angle)), (3, np.sin(angle))):
        for i in range(3):
            table[row + i] = rest.astype(ml_dtypes.bfloat16)
            rest = rest - table[row + i].astype(np.float64)
    return table


def split(x):
    high = x.astype(BF16)
    return high, (x - high.astype(F32)).astype(BF16)


def dot(a, b, contract, precision=None):
    return lax.dot_general(
        a, b, (contract, ((), ())), precision=precision, preferred_element_type=F32
    )


def kernel(
    total_pairs,
    pair_c, pair_v, energy_c, energy_v,
    psi_c, psi_v, wz, wy, wx, g_index,
    rows_out, columns_out,
    band_v, band_c0, band_c1, band_c2, band_c3, density, z_part, y_part, point_data,
    own, core_in, sums, x_out, x_in, chip_out, chip_in, block, z_blocks, row_blocks, col_blocks, load,
    x_send, x_recv, core_send, core_recv, chip_send, chip_recv, z_send, z_recv,
    row_send, row_recv, plane_send, plane_recv, relay_send, relay_recv,
):
    f, g = lax.axis_index("fft"), lax.axis_index("grp")
    core, chip, z = f % 2, f // 2, f // 4
    x = chip % 2
    sibling = f + 1 - 2 * core
    partner = chip + 1 - 2 * x

    band_c = (band_c0, band_c1, band_c2, band_c3)

    def piece(i):
        rows = pl.ds(i * PIECE, PIECE)
        return pltpu.make_async_copy(psi_c.at[:, rows], band_c[i], load.at[8 + i])

    copy_v = pltpu.make_async_copy(psi_v, band_v, load.at[1])
    copy_v.start()
    for i in range(LOADS):
        piece(i).start()

    stores = [
        pltpu.make_async_copy(row_blocks, rows_out, load.at[2]),
        pltpu.make_async_copy(col_blocks.at[core], columns_out.at[core], load.at[3]),
        pltpu.make_async_copy(col_blocks.at[1 - core], columns_out.at[1 - core], load.at[4]),
    ]

    def remote(src, dst, send, recv, to):
        return pltpu.make_async_remote_copy(
            src_ref=src, dst_ref=dst, send_sem=send, recv_sem=recv,
            device_id=to, device_id_type=MESH,
        )

    barrier = pltpu.get_barrier_semaphore()
    pl.semaphore_signal(barrier, 1, device_id=(sibling, g), device_id_type=MESH)

    def greet_chip(k, _):
        to = ((2 * chip + 2 * k) % 32 + core, g)
        pl.semaphore_signal(barrier, 1, device_id=to, device_id_type=MESH)
        return 0

    lax.fori_loop(1, CHIPS, greet_chip, 0)

    def greet_plane(k, _):
        to = (z * 4 + (k % 2) * 2 + core, (g + k // 2) % 8)
        pl.semaphore_signal(barrier, 1, device_id=to, device_id_type=MESH)
        return 0

    lax.fori_loop(2, 16, greet_plane, 0)

    turn_row = lax.broadcasted_iota(jnp.int32, (NG, 2 * CHIP_POINTS), 0)

    def prepare(j, _):
        lanes = pl.ds(pl.multiple_of(j * CHIP_POINTS, 128), CHIP_POINTS)
        points = g_index[0:1, lanes]
        a, b, c = points >> 12, (points >> 6) & 63, points & 63
        mirror = c > 32
        a = jnp.where(mirror, (NG - a) & 63, a)
        b = jnp.where(mirror, (NG - b) & 63, b)
        c = jnp.where(mirror, NG - c, c)
        turns = jnp.concatenate([(a * (2 * f)) & 63, (a * (2 * f + 1)) & 63], 1)
        phase = dot(wx[...], jnp.where(turn_row == turns, BF16(1), BF16(0)), ((1,), (0,)))
        cos = phase[0:1] + (phase[1:2] + phase[2:3])
        sin = phase[3:4] + (phase[4:5] + phase[5:6])
        sign = jnp.where(mirror, -1.0, 1.0)
        first, second = slice(0, CHIP_POINTS), slice(CHIP_POINTS, 2 * CHIP_POINTS)
        point_data[:, lanes] = jnp.concatenate([
            cos[:, first], sin[:, first], cos[:, second], sin[:, second],
            sign, (c * NG + b).astype(F32), sign, sign,
        ], 0)
        return 0

    lax.fori_loop(0, CHIPS, prepare, 0)

    column = lax.broadcasted_iota(jnp.int32, (8, BOTH), 1)
    column = jnp.where(column >= PAIRS, column - PAIRS, column)

    def gaps(p, gap):
        return jnp.where(column == p, energy_c[pair_c[p]] - energy_v[pair_v[p]], gap)

    gap = lax.fori_loop(0, PAIRS, gaps, jnp.ones((8, BOTH), F32))
    factor = jnp.sqrt(2.0 / gap) * (total_pairs ** (-0.25) * NG ** (-1.5))

    copy_v.wait()

    def along_z(i, size):
        lines = []
        for t in range(2):
            lines.append(jnp.concatenate([
                density[pl.ds(4 * i + 2 * t + n, PAIRS, stride=NG), :] for n in range(2)
            ], 0))
        high, low = split(jnp.concatenate(lines, 1))
        lines = jnp.concatenate([high, low, high], 1)
        result = dot(wz[...], lines, ((1,), (1,))).reshape(HALF_C, 8, BOTH) * factor
        start = pl.multiple_of(8 * i, 8)
        z_part[:, pl.ds(start, 8), 0:BOTH] = result
        return size + jnp.abs(result)

    size = jnp.zeros((HALF_C, 8, BOTH), F32)
    for part in range(LOADS):
        piece(part).wait()

        def multiply(p, _):
            rows = pl.ds(part * PIECE, PIECE)
            start = pl.multiple_of(p * NG + part * PIECE, PIECE)
            density[pl.ds(start, PIECE), :] = (
                band_v[pair_v[p], rows].astype(F32) * band_c[part][pair_c[p]].astype(F32)
            )
            return 0

        lax.fori_loop(0, PAIRS, multiply, 0, unroll=4)
        for i in range(PIECE // 4):
            size = along_z(part * (PIECE // 4) + i, size)

    size = jnp.max(jnp.sum(size, 1), 0, keepdims=True)
    most = jnp.maximum(jnp.max(size, 1, keepdims=True), 1e-30)
    size = jnp.max(size[:, 0:PAIRS] + size[:, PAIRS:], 1, keepdims=True)
    bound_rows = jnp.broadcast_to(jnp.maximum(size, 1e-30), (8, 128))
    fit = 400.0 / most

    lane = lax.broadcasted_iota(jnp.int32, (BOTH, 128), 1)

    def along_y(k, _):
        lines = jnp.concatenate([z_part[2 * k + n].T[0:BOTH] for n in range(2)], 0)
        high, low = split(lines)
        result = dot(jnp.concatenate([high, low, high], 1), wy[...], ((1,), (0,)))
        first, second = result[0:BOTH], result[BOTH:]
        real = jnp.where(lane < NG, first, pltpu.roll(second, NG, 1))
        imag = jnp.where(lane < NG, pltpu.roll(first, NG, 1), second)
        rest = jnp.concatenate([real, imag], 0) * fit
        start = pl.multiple_of(128 * k, 128)
        for i in range(3):
            piece = rest.astype(FP8)
            y_part[2 * BOTH * i:2 * BOTH * (i + 1), pl.ds(start, 128)] = piece
            rest = rest - piece.astype(F32)
        return 0

    lax.fori_loop(0, HALF_C // 2, along_y, 0, unroll=HALF_C // 2)

    half_lane = lax.broadcasted_iota(jnp.int32, (PAIRS, 128), 1) < NG
    key_row = lax.broadcasted_iota(jnp.int16, (KEYS, WIDE), 0)
    tail = lax.broadcasted_iota(jnp.int32, (128, 128), 0) >= 120
    unfit = most / 400.0

    pl.semaphore_wait(barrier, 30)

    def to_sibling(j):
        return remote(
            own.at[1 - core, j], core_in.at[j], core_send.at[j], core_recv.at[j], (sibling, g)
        )

    def to_chip(j):
        return remote(
            chip_out.at[j], chip_in.at[chip], chip_send.at[j], chip_recv.at[chip], (2 * j + core, g)
        )

    def layer_of(k):
        return (z + (4 - (k + 1) // 2) * (2 * (k % 2) - 1) + 8) % 8

    def arrive(k):
        for n in range(2):
            to_sibling(2 * layer_of(k) + n).wait_recv()

    def rounded(total, bound):
        level = jnp.floor(jnp.log2(bound * 1.001)) + 1.0
        total = jnp.where(tail, level, jnp.floor(total * jnp.exp2(15.0 - level) + 0.5))
        return total.astype(jnp.int32).astype(jnp.int16)

    def add_core(k):
        for n in range(2):
            j = 2 * layer_of(k) + n
            total = own[core, j] + core_in[j]
            chip_out[j] = rounded(total, total[120:121])

    def to_partner(m):
        return remote(
            x_out.at[m], x_in.at[m], x_send.at[m], x_recv.at[m], (2 * partner + core, g)
        )

    def add_far(k):
        m = layer_of(k)
        mine, other = 2 * m + x, 2 * m + 1 - x
        total = own[core, other] + core_in[other]
        x_out[m] = rounded(total, total[120:121])
        to_partner(m).start()
        sums[m] = own[core, mine] + core_in[mine]

    def join(k):
        m = layer_of(k)
        to_partner(m).wait_recv()
        theirs = x_in[m].astype(jnp.int32).astype(F32)
        theirs_level = theirs[120:121]
        total = sums[m] + theirs * jnp.exp2(theirs_level - 15.0)
        bound = sums[m, 120:121] + jnp.exp2(theirs_level)
        chip_out[2 * m + x] = rounded(total, bound)
        to_chip(2 * m + x).start()

    def select(k):
        m = layer_of(k)
        data = point_data[:, pl.ds(pl.multiple_of(m * WIDE, 128), WIDE)]
        key = data[5:6].astype(jnp.int32).astype(jnp.int16)
        chosen = jnp.where(key_row == key, BF16(1), BF16(0)).astype(FP8)
        picked = dot(y_part[...], chosen, ((1,), (0,)))
        picked = picked[0:2 * BOTH] + (picked[2 * BOTH:4 * BOTH] + picked[4 * BOTH:])
        re0, re1, im0, im1 = (picked[i * PAIRS:(i + 1) * PAIRS] for i in range(4))
        turned = data * unfit
        cos0, sin0, cos1, sin1 = (turned[i:i + 1] for i in range(4))
        signed = turned * data[4:5]
        cos0_im, sin0_im, cos1_im, sin1_im = (signed[i:i + 1] for i in range(4))
        real = cos0 * re0 + sin0 * im0 + cos1 * re1 + sin1 * im1
        imag = cos0_im * im0 - sin0_im * re0 + cos1_im * im1 - sin1_im * re1
        for n in range(2):
            at = n * CHIP_POINTS
            middle_re, middle_im = real[:, at + 128:at + 256], imag[:, at + 128:at + 256]
            for side in range(2):
                if side == 0:
                    middle = jnp.where(half_lane, middle_re, pltpu.roll(middle_im, NG, 1))
                else:
                    middle = jnp.where(half_lane, pltpu.roll(middle_re, NG, 1), middle_im)
                lanes = slice(at + 256 * side, at + 256 * side + 128)
                own[side, 2 * m + n] = jnp.concatenate(
                    [real[:, lanes], imag[:, lanes], middle, bound_rows], 0
                )

    def hand_over(k):
        for n in range(2):
            to_sibling(2 * layer_of(k) + n).start()

    def send(k):
        for n in range(2):
            to_chip(2 * layer_of(k) + n).start()

    def scaled(slab):
        slab = slab.astype(jnp.int32).astype(F32)
        return slab * jnp.exp2(slab[120:121] - 15.0)

    def chip_arrives(j, total):
        remote(
            chip_out.at[j], chip_in.at[j], chip_send.at[j], chip_recv.at[j], (2 * j + core, g)
        ).wait_recv()
        return total + scaled(chip_in[j])

    def add_chips(k, total):
        layer = (2 * z - layer_of(k) + 8) % 8
        return chip_arrives(2 * layer + 1, chip_arrives(2 * layer, total))

    def add_joined(k, total):
        return chip_arrives(2 * ((2 * z - layer_of(k) + 8) % 8) + x, total)

    def loop(first, last, body):
        def run(k, _):
            body(k)
            return 0

        lax.fori_loop(first, last, run, 0)

    def step(k, far, joins):
        select(k)
        hand_over(k)
        arrive(k - 1)
        if far:
            add_far(k - 1)
        else:
            add_core(k - 1)
            send(k - 1)
        if joins:
            join(k - JOIN_LAG)

    select(0)
    hand_over(0)
    step(1, False, False)
    loop(2, 1 + JOIN_LAG, lambda k: step(k, True, False))
    loop(1 + JOIN_LAG, 6, lambda k: step(k, True, True))
    loop(6, 8, lambda k: step(k, False, True))
    arrive(7)
    add_core(7)
    to_chip(2 * z + 1 - x).start()
    loop(8 - JOIN_LAG, 5, join)
    total = add_chips(0, scaled(chip_out[chip]))
    total = lax.fori_loop(1, 5, add_joined, total)
    total = lax.fori_loop(5, 7, add_chips, total)
    total = chip_arrives(partner, total)
    block[...] = jnp.where(tail, 0.0, total).astype(BF16)

    def to_z(k):
        other = (z + k) % 8
        return remote(
            block, z_blocks.at[z], z_send.at[other], z_recv.at[z], (other * 4 + x * 2 + core, g)
        )

    def to_row(k):
        other = (g + k) % 8
        return remote(block, row_blocks.at[g], row_send.at[other], row_recv.at[g], (f, other))

    def near(k):
        return (k + 1) // 2 * (1 - 2 * (k % 2)) + 8

    def send_z(k, _):
        to_z(near(k)).start()
        return 0

    def send_row(k, _):
        to_row(k).start()
        return 0

    lax.fori_loop(1, 8, send_z, 0)
    lax.fori_loop(1, 8, send_row, 0)
    z_blocks[z] = block[...]
    row_blocks[g] = block[...]

    def to_plane(layer, to_x):
        return remote(
            z_blocks.at[layer], col_blocks.at[core, x, g],
            plane_send.at[layer, to_x], plane_recv.at[x, g], (z * 4 + to_x * 2 + core, layer),
        )

    def stays(layer, to_x):
        return jnp.logical_and(layer == g, to_x == x)

    def spread(k, _):
        layer = (z + near(k)) % 8

        @pl.when(k > 0)
        def _():
            remote(
                block, z_blocks.at[layer], z_send.at[layer], z_recv.at[layer],
                (layer * 4 + x * 2 + core, g),
            ).wait_recv()

        for to_x in range(2):
            @pl.when(stays(layer, to_x))
            def _():
                col_blocks[core, x, g] = z_blocks[layer]

            @pl.when(jnp.logical_not(stays(layer, to_x)))
            def _():
                to_plane(layer, to_x).start()

        return 0

    spread(0, 0)
    loop(0, CHIPS, lambda j: to_sibling(j).wait_send())
    for k in (0, 5, 6):
        for n in range(2):
            to_chip(2 * layer_of(k) + n).wait_send()
    for k in range(1, 5):
        to_partner(layer_of(k)).wait_send()
        to_chip(2 * layer_of(k) + x).wait_send()
    to_chip(2 * z + 1 - x).wait_send()
    lax.fori_loop(1, 8, spread, 0)

    def drain_blocks(k, _):
        to_z(k).wait_send()
        to_row(k).wait_send()
        return 0

    lax.fori_loop(1, 8, drain_blocks, 0)

    def row_arrives(k, _):
        other = (g + k) % 8
        remote(
            block, row_blocks.at[other], row_send.at[other], row_recv.at[other], (f, other)
        ).wait_recv()
        return 0

    lax.fori_loop(1, 8, row_arrives, 0)
    stores[0].start()

    def relay(side, from_x, from_g):
        return remote(
            col_blocks.at[side, from_x, from_g], col_blocks.at[side, from_x, from_g],
            relay_send.at[from_x, from_g], relay_recv.at[from_x, from_g], (sibling, g),
        )

    def pass_on(k, _):
        from_x, from_g = (x + k) % 2, (g + k // 2) % 8

        @pl.when(k > 0)
        def _():
            remote(
                z_blocks.at[0], col_blocks.at[core, from_x, from_g],
                plane_send.at[0, 0], plane_recv.at[from_x, from_g],
                (z * 4 + from_x * 2 + core, from_g),
            ).wait_recv()

        relay(core, from_x, from_g).start()
        return 0

    lax.fori_loop(0, 16, pass_on, 0)

    def drain_plane(k, _):
        @pl.when(jnp.logical_not(stays(k // 2, k % 2)))
        def _():
            to_plane(k // 2, k % 2).wait_send()

        return 0

    lax.fori_loop(0, 16, drain_plane, 0)

    stores[1].start()

    def relay_arrives(k, _):
        relay(1 - core, k % 2, k // 2).wait_recv()
        return 0

    lax.fori_loop(0, 16, relay_arrives, 0)
    stores[2].start()

    loop(0, 16, lambda k: relay(core, k % 2, k // 2).wait_send())
    stores[0].wait()
    stores[1].wait()
    stores[2].wait()

def product_kernel(rows_in, columns_in, chi_real, chi_imag):
    core = lax.axis_index("fft") % 2
    half_lane = lax.broadcasted_iota(jnp.int32, (8 * PAIRS, 128), 1) < NG

    def gather(read):
        blocks = [read(i).astype(F32) for i in range(8)]
        return tuple(
            jnp.concatenate([b[s * PAIRS:(s + 1) * PAIRS] for b in blocks], 0) for s in range(3)
        )

    real, imag, middle = gather(lambda i: rows_in[i])
    full = jnp.concatenate([real, imag], 0).astype(BF16)
    half = jnp.concatenate([middle, pltpu.roll(middle, NG, 1)], 0)[:, 0:NG].astype(BF16)
    full_row = pl.multiple_of(core * NG, NG)
    half_row = pl.multiple_of((1 - core) * 128, NG)
    real0, imag0, middle0 = gather(lambda i: columns_in[0, 0, i])
    real2, imag2, middle2 = gather(lambda i: columns_in[1, 0, i])
    real1 = jnp.where(half_lane, middle0, pltpu.roll(middle2, NG, 1))
    imag1 = jnp.where(half_lane, pltpu.roll(middle0, NG, 1), middle2)
    real = jnp.concatenate([real0, real1, real2], 1)
    imag = jnp.concatenate([imag0, imag1, imag2], 1)
    right_sum = jnp.concatenate([real, imag], 0).astype(BF16)
    right_cross = jnp.concatenate([imag, -real], 0).astype(BF16)
    for left, rows in ((full, pl.ds(full_row, 128)), (half, pl.ds(half_row, NG))):
        chi_real[rows, :] = -dot(left, right_sum, ((0,), (0,)))
        chi_imag[rows, :] = dot(left, right_cross, ((0,), (0,)))


def product(rows, columns, shape):
    count, width = shape.shape
    out = pl.BlockSpec((count, CHIP_POINTS), lambda side: (0, side))
    return pl.pallas_call(
        product_kernel,
        grid=(width // CHIP_POINTS,),
        out_shape=(shape, shape),
        in_specs=[
            pl.BlockSpec((8, 128, 128), lambda side: (0, 0, 0)),
            pl.BlockSpec((2, 1, 8, 128, 128), lambda side: (0, side, 0, 0, 0)),
        ],
        out_specs=(out, out),
        compiler_params=pltpu.CompilerParams(vmem_limit_bytes=56 * 1024 * 1024),
    )(rows, columns)


def per_device(
    psi_valence,
    psi_conduction,
    energy_valence,
    energy_conduction,
    pair_valence,
    pair_conduction,
    g_index,
):
    def tiles(psi):
        bands = psi.shape[0]
        return psi.reshape(bands, 2, 32, 128).transpose(0, 2, 1, 3).reshape(bands, NG, 128)

    psi_c, psi_v = tiles(psi_conduction), tiles(psi_valence)
    points = g_index.shape[0]
    shape = jax.ShapeDtypeStruct(
        (points // lax.axis_size("fft"), points // lax.axis_size("grp")), F32
    )
    smem = pl.BlockSpec(memory_space=pltpu.SMEM)
    vmem = pl.BlockSpec(memory_space=pltpu.VMEM)
    anywhere = pl.BlockSpec(memory_space=pl.ANY)
    dma = pltpu.SemaphoreType.DMA

    slabs = pltpu.VMEM((CHIPS, 128, 128), jnp.int16)
    blocks = pltpu.VMEM((8, 128, 128), BF16)
    rows, columns = pl.pallas_call(
        functools.partial(kernel, PAIRS * lax.axis_size("grp")),
        out_shape=(
            jax.ShapeDtypeStruct((8, 128, 128), BF16),
            jax.ShapeDtypeStruct((2, 2, 8, 128, 128), BF16),
        ),
        in_specs=[smem] * 4 + [anywhere] * 2 + [vmem] * 4,
        out_specs=(anywhere, anywhere),
        scratch_shapes=[
            pltpu.VMEM(psi_v.shape, BF16),
            *[pltpu.VMEM((psi_c.shape[0], PIECE, 128), BF16)] * LOADS,
            pltpu.VMEM((PAIRS * NG, 128), F32),
            pltpu.VMEM((HALF_C, 128, 128), F32),
            pltpu.VMEM((6 * BOTH, KEYS), FP8),
            pltpu.VMEM((8, points), F32),
            pltpu.VMEM((2, CHIPS, 128, 128), F32),
            pltpu.VMEM((CHIPS, 128, 128), F32),
            pltpu.VMEM((8, 128, 128), F32),
            pltpu.VMEM((8, 128, 128), jnp.int16), pltpu.VMEM((8, 128, 128), jnp.int16),
            slabs, slabs,
            pltpu.VMEM((128, 128), BF16),
            blocks, blocks,
            pltpu.VMEM((2, 2, 8, 128, 128), BF16),
            dma((8 + LOADS,)),
            dma((8,)), dma((8,)),
            dma((CHIPS,)), dma((CHIPS,)), dma((CHIPS,)), dma((CHIPS,)),
            dma((8,)), dma((8,)), dma((8,)), dma((8,)),
            dma((8, 2)), dma((2, 8)), dma((2, 8)), dma((2, 8)),
        ],
        compiler_params=pltpu.CompilerParams(
            collective_id=0, has_side_effects=True, vmem_limit_bytes=62 * 1024 * 1024
        ),
    )(
        pair_conduction, pair_valence, energy_conduction, energy_valence, psi_c, psi_v,
        jnp.asarray(table_z()), jnp.asarray(table_y()), jnp.asarray(table_x()),
        g_index.reshape(1, -1),
    )
    return product(rows, columns, shape)


def solution(mesh):
    placed = (P(None, "fft", None), P(None, "fft", None), P(), P(), P("grp"), P("grp"), P())
    return jax.shard_map(
        per_device,
        mesh=mesh,
        in_specs=placed,
        out_specs=(P("fft", "grp"), P("fft", "grp")),
        check_vma=False,
    )
```

```python
import functools
import math

import jax
import jax.numpy as jnp
import ml_dtypes
import numpy as np
from jax import lax
from jax.experimental import pallas as pl
from jax.experimental.pallas import tpu as pltpu
from jax.sharding import PartitionSpec as P

NG = 64
HALF_C = 34
KEYS = HALF_C * NG
PAIRS = 40
BOTH = 2 * PAIRS
CHIPS = 16
JOIN_LAG = 3
LOADS = 4
PIECE = NG // LOADS
CHIP_POINTS = 384
WIDE = 2 * CHIP_POINTS
BF16 = jnp.bfloat16
F32 = jnp.float32
FP8 = jnp.float8_e4m3fn
MESH = pl.DeviceIdType.MESH


def split_table(table):
    high = table.astype(ml_dtypes.bfloat16)
    low = (table - high.astype(np.float64)).astype(ml_dtypes.bfloat16)
    return high, low


def table_z():
    c, z = np.arange(33)[:, None], np.arange(NG)[None, :]
    angle = 2 * np.pi * ((c * z) % NG) / NG
    table = np.zeros((HALF_C, 4, 2, 4, NG))
    for y in range(4):
        table[:33, y, 0, y] = np.cos(angle)
        table[:33, y, 1, y] = -np.sin(angle)
    high, low = split_table(table.reshape(HALF_C * 8, 4 * NG))
    return np.concatenate([high, high, low], 1)


def table_y():
    y, b = np.arange(NG)[:, None], np.arange(NG)[None, :]
    angle = 2 * np.pi * ((y * b) % NG) / NG
    table = np.zeros((NG, 2, 2, NG))
    table[:, 0, 0], table[:, 0, 1] = np.cos(angle), -np.sin(angle)
    table[:, 1, 0], table[:, 1, 1] = np.sin(angle), np.cos(angle)
    high, low = split_table(table.reshape(2 * NG, 2 * NG))
    return np.concatenate([high, high, low], 0)


def table_x():
    angle = 2 * np.pi * np.arange(NG) / NG
    table = np.zeros((16, NG), ml_dtypes.bfloat16)
    for row, rest in ((0, np.cos(angle)), (3, np.sin(angle))):
        for i in range(3):
            table[row + i] = rest.astype(ml_dtypes.bfloat16)
            rest = rest - table[row + i].astype(np.float64)
    return table


def split(x):
    high = x.astype(BF16)
    return high, (x - high.astype(F32)).astype(BF16)


def dot(a, b, contract, precision=None):
    return lax.dot_general(
        a, b, (contract, ((), ())), precision=precision, preferred_element_type=F32
    )


def kernel(
    total_pairs,
    pair_c, pair_v, energy_c, energy_v,
    psi_c, psi_v, wz, wy, wx, g_index,
    rows_out, columns_out,
    band_v, band_c0, band_c1, band_c2, band_c3, density, z_part, y_part, point_data,
    own, core_in, sums, x_out, x_in, chip_out, chip_in, block, z_blocks, row_blocks, col_blocks, load,
    x_send, x_recv, core_send, core_recv, chip_send, chip_recv, z_send, z_recv,
    row_send, row_recv, plane_send, plane_recv, relay_send, relay_recv,
):
    f, g = lax.axis_index("fft"), lax.axis_index("grp")
    core, chip, z = f % 2, f // 2, f // 4
    x = chip % 2
    sibling = f + 1 - 2 * core
    partner = chip + 1 - 2 * x

    band_c = (band_c0, band_c1, band_c2, band_c3)

    def piece(i):
        rows = pl.ds(i * PIECE, PIECE)
        return pltpu.make_async_copy(psi_c.at[:, rows], band_c[i], load.at[8 + i])

    copy_v = pltpu.make_async_copy(psi_v, band_v, load.at[1])
    copy_v.start()
    for i in range(LOADS):
        piece(i).start()

    stores = [
        pltpu.make_async_copy(row_blocks, rows_out, load.at[2]),
        pltpu.make_async_copy(col_blocks.at[core], columns_out.at[core], load.at[3]),
        *(
            pltpu.make_async_copy(
                col_blocks.at[1 - core, n], columns_out.at[1 - core, n], load.at[4 + n]
            )
            for n in range(2)
        ),
    ]

    def remote(src, dst, send, recv, to):
        return pltpu.make_async_remote_copy(
            src_ref=src, dst_ref=dst, send_sem=send, recv_sem=recv,
            device_id=to, device_id_type=MESH,
        )

    barrier = pltpu.get_barrier_semaphore()
    pl.semaphore_signal(barrier, 1, device_id=(sibling, g), device_id_type=MESH)

    def greet_chip(k, _):
        to = ((2 * chip + 2 * k) % 32 + core, g)
        pl.semaphore_signal(barrier, 1, device_id=to, device_id_type=MESH)
        return 0

    lax.fori_loop(1, CHIPS, greet_chip, 0)

    def greet_plane(k, _):
        to = (z * 4 + (k % 2) * 2 + core, (g + k // 2) % 8)
        pl.semaphore_signal(barrier, 1, device_id=to, device_id_type=MESH)
        return 0

    lax.fori_loop(2, 16, greet_plane, 0)

    turn_row = lax.broadcasted_iota(jnp.int32, (NG, 2 * CHIP_POINTS), 0)

    def prepare(j, _):
        lanes = pl.ds(pl.multiple_of(j * CHIP_POINTS, 128), CHIP_POINTS)
        points = g_index[0:1, lanes]
        a, b, c = points >> 12, (points >> 6) & 63, points & 63
        mirror = c > 32
        a = jnp.where(mirror, (NG - a) & 63, a)
        b = jnp.where(mirror, (NG - b) & 63, b)
        c = jnp.where(mirror, NG - c, c)
        turns = jnp.concatenate([(a * (2 * f)) & 63, (a * (2 * f + 1)) & 63], 1)
        phase = dot(wx[...], jnp.where(turn_row == turns, BF16(1), BF16(0)), ((1,), (0,)))
        cos = phase[0:1] + (phase[1:2] + phase[2:3])
        sin = phase[3:4] + (phase[4:5] + phase[5:6])
        sign = jnp.where(mirror, -1.0, 1.0)
        first, second = slice(0, CHIP_POINTS), slice(CHIP_POINTS, 2 * CHIP_POINTS)
        point_data[:, lanes] = jnp.concatenate([
            cos[:, first], sin[:, first], cos[:, second], sin[:, second],
            sign, (c * NG + b).astype(F32), sign, sign,
        ], 0)
        return 0

    lax.fori_loop(0, CHIPS, prepare, 0)

    column = lax.broadcasted_iota(jnp.int32, (8, BOTH), 1)
    column = jnp.where(column >= PAIRS, column - PAIRS, column)

    def gaps(p, gap):
        return jnp.where(column == p, energy_c[pair_c[p]] - energy_v[pair_v[p]], gap)

    gap = lax.fori_loop(0, PAIRS, gaps, jnp.ones((8, BOTH), F32))
    factor = jnp.sqrt(2.0 / gap) * (total_pairs ** (-0.25) * NG ** (-1.5))

    copy_v.wait()

    def along_z(i, size):
        lines = []
        for t in range(2):
            lines.append(jnp.concatenate([
                density[pl.ds(4 * i + 2 * t + n, PAIRS, stride=NG), :] for n in range(2)
            ], 0))
        high, low = split(jnp.concatenate(lines, 1))
        lines = jnp.concatenate([high, low, high], 1)
        result = dot(wz[...], lines, ((1,), (1,))).reshape(HALF_C, 8, BOTH) * factor
        start = pl.multiple_of(8 * i, 8)
        z_part[:, pl.ds(start, 8), 0:BOTH] = result
        return size + jnp.abs(result)

    size = jnp.zeros((HALF_C, 8, BOTH), F32)
    for part in range(LOADS):
        piece(part).wait()

        def multiply(p, _):
            rows = pl.ds(part * PIECE, PIECE)
            start = pl.multiple_of(p * NG + part * PIECE, PIECE)
            density[pl.ds(start, PIECE), :] = (
                band_v[pair_v[p], rows].astype(F32) * band_c[part][pair_c[p]].astype(F32)
            )
            return 0

        lax.fori_loop(0, PAIRS, multiply, 0, unroll=4)
        for i in range(PIECE // 4):
            size = along_z(part * (PIECE // 4) + i, size)

    size = jnp.max(jnp.sum(size, 1), 0, keepdims=True)
    most = jnp.maximum(jnp.max(size, 1, keepdims=True), 1e-30)
    size = jnp.max(size[:, 0:PAIRS] + size[:, PAIRS:], 1, keepdims=True)
    bound_rows = jnp.broadcast_to(jnp.maximum(size, 1e-30), (8, 128))
    fit = 400.0 / most

    lane = lax.broadcasted_iota(jnp.int32, (BOTH, 128), 1)

    def along_y(k, _):
        lines = jnp.concatenate([z_part[2 * k + n].T[0:BOTH] for n in range(2)], 0)
        high, low = split(lines)
        result = dot(jnp.concatenate([high, low, high], 1), wy[...], ((1,), (0,)))
        first, second = result[0:BOTH], result[BOTH:]
        real = jnp.where(lane < NG, first, pltpu.roll(second, NG, 1))
        imag = jnp.where(lane < NG, pltpu.roll(first, NG, 1), second)
        rest = jnp.concatenate([real, imag], 0) * fit
        start = pl.multiple_of(128 * k, 128)
        for i in range(3):
            piece = rest.astype(FP8)
            y_part[2 * BOTH * i:2 * BOTH * (i + 1), pl.ds(start, 128)] = piece
            rest = rest - piece.astype(F32)
        return 0

    lax.fori_loop(0, HALF_C // 2, along_y, 0, unroll=HALF_C // 2)

    half_lane = lax.broadcasted_iota(jnp.int32, (PAIRS, 128), 1) < NG
    key_row = lax.broadcasted_iota(jnp.int16, (KEYS, WIDE), 0)
    tail = lax.broadcasted_iota(jnp.int32, (128, 128), 0) >= 120
    unfit = most / 400.0

    pl.semaphore_wait(barrier, 30)

    def to_sibling(j):
        return remote(
            own.at[1 - core, j], core_in.at[j], core_send.at[j], core_recv.at[j], (sibling, g)
        )

    def to_chip(j):
        return remote(
            chip_out.at[j], chip_in.at[chip], chip_send.at[j], chip_recv.at[chip], (2 * j + core, g)
        )

    def layer_of(k):
        return (z + (4 - (k + 1) // 2) * (2 * (k % 2) - 1) + 8) % 8

    def arrive(k):
        for n in range(2):
            to_sibling(2 * layer_of(k) + n).wait_recv()

    def rounded(total, bound):
        level = jnp.floor(jnp.log2(bound * 1.001)) + 1.0
        total = jnp.where(tail, level, jnp.floor(total * jnp.exp2(15.0 - level) + 0.5))
        return total.astype(jnp.int32).astype(jnp.int16)

    def add_core(k):
        for n in range(2):
            j = 2 * layer_of(k) + n
            total = own[core, j] + core_in[j]
            chip_out[j] = rounded(total, total[120:121])

    def to_partner(m):
        return remote(
            x_out.at[m], x_in.at[m], x_send.at[m], x_recv.at[m], (2 * partner + core, g)
        )

    def add_far(k):
        m = layer_of(k)
        mine, other = 2 * m + x, 2 * m + 1 - x
        total = own[core, other] + core_in[other]
        x_out[m] = rounded(total, total[120:121])
        to_partner(m).start()
        sums[m] = own[core, mine] + core_in[mine]

    def join(k):
        m = layer_of(k)
        to_partner(m).wait_recv()
        theirs = x_in[m].astype(jnp.int32).astype(F32)
        theirs_level = theirs[120:121]
        total = sums[m] + theirs * jnp.exp2(theirs_level - 15.0)
        bound = sums[m, 120:121] + jnp.exp2(theirs_level)
        chip_out[2 * m + x] = rounded(total, bound)
        to_chip(2 * m + x).start()

    def select(k):
        m = layer_of(k)
        data = point_data[:, pl.ds(pl.multiple_of(m * WIDE, 128), WIDE)]
        key = data[5:6].astype(jnp.int32).astype(jnp.int16)
        chosen = jnp.where(key_row == key, BF16(1), BF16(0)).astype(FP8)
        picked = dot(y_part[...], chosen, ((1,), (0,)))
        picked = picked[0:2 * BOTH] + (picked[2 * BOTH:4 * BOTH] + picked[4 * BOTH:])
        re0, re1, im0, im1 = (picked[i * PAIRS:(i + 1) * PAIRS] for i in range(4))
        turned = data * unfit
        cos0, sin0, cos1, sin1 = (turned[i:i + 1] for i in range(4))
        signed = turned * data[4:5]
        cos0_im, sin0_im, cos1_im, sin1_im = (signed[i:i + 1] for i in range(4))
        real = cos0 * re0 + sin0 * im0 + cos1 * re1 + sin1 * im1
        imag = cos0_im * im0 - sin0_im * re0 + cos1_im * im1 - sin1_im * re1
        for n in range(2):
            at = n * CHIP_POINTS
            middle_re, middle_im = real[:, at + 128:at + 256], imag[:, at + 128:at + 256]
            for side in range(2):
                if side == 0:
                    middle = jnp.where(half_lane, middle_re, pltpu.roll(middle_im, NG, 1))
                else:
                    middle = jnp.where(half_lane, pltpu.roll(middle_re, NG, 1), middle_im)
                lanes = slice(at + 256 * side, at + 256 * side + 128)
                own[side, 2 * m + n] = jnp.concatenate(
                    [real[:, lanes], imag[:, lanes], middle, bound_rows], 0
                )

    def hand_over(k):
        for n in range(2):
            to_sibling(2 * layer_of(k) + n).start()

    def send(k):
        for n in range(2):
            to_chip(2 * layer_of(k) + n).start()

    def scaled(slab):
        slab = slab.astype(jnp.int32).astype(F32)
        return slab * jnp.exp2(slab[120:121] - 15.0)

    def chip_arrives(j, total):
        remote(
            chip_out.at[j], chip_in.at[j], chip_send.at[j], chip_recv.at[j], (2 * j + core, g)
        ).wait_recv()
        return total + scaled(chip_in[j])

    def add_chips(k, total):
        layer = (2 * z - layer_of(k) + 8) % 8
        return chip_arrives(2 * layer + 1, chip_arrives(2 * layer, total))

    def add_joined(k, total):
        return chip_arrives(2 * ((2 * z - layer_of(k) + 8) % 8) + x, total)

    def loop(first, last, body):
        def run(k, _):
            body(k)
            return 0

        lax.fori_loop(first, last, run, 0)

    def step(k, far, joins):
        select(k)
        hand_over(k)
        arrive(k - 1)
        if far:
            add_far(k - 1)
        else:
            add_core(k - 1)
            send(k - 1)
        if joins:
            join(k - JOIN_LAG)

    select(0)
    hand_over(0)
    step(1, False, False)
    loop(2, 1 + JOIN_LAG, lambda k: step(k, True, False))
    loop(1 + JOIN_LAG, 6, lambda k: step(k, True, True))
    loop(6, 8, lambda k: step(k, False, True))
    arrive(7)
    add_core(7)
    to_chip(2 * z + 1 - x).start()
    loop(8 - JOIN_LAG, 5, join)
    total = add_chips(0, scaled(chip_out[chip]))
    total = lax.fori_loop(1, 5, add_joined, total)
    total = lax.fori_loop(5, 7, add_chips, total)
    total = chip_arrives(partner, total)
    block[...] = jnp.where(tail, 0.0, total).astype(BF16)

    def to_z(k):
        other = (z + k) % 8
        return remote(
            block, z_blocks.at[z], z_send.at[other], z_recv.at[z], (other * 4 + x * 2 + core, g)
        )

    def to_row(k):
        other = (g + k) % 8
        return remote(block, row_blocks.at[g], row_send.at[other], row_recv.at[g], (f, other))

    def near(k):
        return (k + 1) // 2 * (1 - 2 * (k % 2)) + 8

    def send_z(k, _):
        to_z(near(k)).start()
        return 0

    def send_row(k, _):
        to_row(k).start()
        return 0

    lax.fori_loop(1, 8, send_z, 0)
    lax.fori_loop(1, 8, send_row, 0)
    z_blocks[z] = block[...]
    row_blocks[g] = block[...]

    def to_plane(layer, to_x):
        return remote(
            z_blocks.at[layer], col_blocks.at[core, x, g],
            plane_send.at[layer, to_x], plane_recv.at[x, g], (z * 4 + to_x * 2 + core, layer),
        )

    def stays(layer, to_x):
        return jnp.logical_and(layer == g, to_x == x)

    def spread(k, _):
        layer = (z + near(k)) % 8

        @pl.when(k > 0)
        def _():
            remote(
                block, z_blocks.at[layer], z_send.at[layer], z_recv.at[layer],
                (layer * 4 + x * 2 + core, g),
            ).wait_recv()

        for to_x in range(2):
            @pl.when(stays(layer, to_x))
            def _():
                col_blocks[core, x, g] = z_blocks[layer]

            @pl.when(jnp.logical_not(stays(layer, to_x)))
            def _():
                to_plane(layer, to_x).start()

        return 0

    spread(0, 0)
    loop(0, CHIPS, lambda j: to_sibling(j).wait_send())
    for k in (0, 5, 6):
        for n in range(2):
            to_chip(2 * layer_of(k) + n).wait_send()
    for k in range(1, 5):
        to_partner(layer_of(k)).wait_send()
        to_chip(2 * layer_of(k) + x).wait_send()
    to_chip(2 * z + 1 - x).wait_send()
    lax.fori_loop(1, 8, spread, 0)

    def drain_blocks(k, _):
        to_z(k).wait_send()
        to_row(k).wait_send()
        return 0

    lax.fori_loop(1, 8, drain_blocks, 0)

    def row_arrives(k, _):
        other = (g + k) % 8
        remote(
            block, row_blocks.at[other], row_send.at[other], row_recv.at[other], (f, other)
        ).wait_recv()
        return 0

    lax.fori_loop(1, 8, row_arrives, 0)
    stores[0].start()

    def relay(side, from_x, from_g):
        return remote(
            col_blocks.at[side, from_x, from_g], col_blocks.at[side, from_x, from_g],
            relay_send.at[from_x, from_g], relay_recv.at[from_x, from_g], (sibling, g),
        )

    def pass_on(k, _):
        from_x, from_g = (x + k) % 2, (g + k // 2) % 8

        @pl.when(k > 0)
        def _():
            remote(
                z_blocks.at[0], col_blocks.at[core, from_x, from_g],
                plane_send.at[0, 0], plane_recv.at[from_x, from_g],
                (z * 4 + from_x * 2 + core, from_g),
            ).wait_recv()

        relay(core, from_x, from_g).start()
        return 0

    lax.fori_loop(0, 16, pass_on, 0)

    def drain_plane(k, _):
        @pl.when(jnp.logical_not(stays(k // 2, k % 2)))
        def _():
            to_plane(k // 2, k % 2).wait_send()

        return 0

    lax.fori_loop(0, 16, drain_plane, 0)

    stores[1].start()

    def relay_arrives(k, _):
        relay(1 - core, k // 8, k % 8).wait_recv()
        return 0

    lax.fori_loop(0, 8, relay_arrives, 0)
    stores[2].start()
    lax.fori_loop(8, 16, relay_arrives, 0)
    stores[3].start()

    loop(0, 16, lambda k: relay(core, k % 2, k // 2).wait_send())
    stores[0].wait()
    stores[1].wait()
    stores[2].wait()
    stores[3].wait()

def product_kernel(rows_in, columns_in, chi_real, chi_imag):
    core = lax.axis_index("fft") % 2
    half_lane = lax.broadcasted_iota(jnp.int32, (8 * PAIRS, 128), 1) < NG

    def gather(read):
        blocks = [read(i).astype(F32) for i in range(8)]
        return tuple(
            jnp.concatenate([b[s * PAIRS:(s + 1) * PAIRS] for b in blocks], 0) for s in range(3)
        )

    real, imag, middle = gather(lambda i: rows_in[i])
    full = jnp.concatenate([real, imag], 0).astype(BF16)
    half = jnp.concatenate([middle, pltpu.roll(middle, NG, 1)], 0)[:, 0:NG].astype(BF16)
    full_row = pl.multiple_of(core * NG, NG)
    half_row = pl.multiple_of((1 - core) * 128, NG)
    real0, imag0, middle0 = gather(lambda i: columns_in[0, 0, i])
    real2, imag2, middle2 = gather(lambda i: columns_in[1, 0, i])
    real1 = jnp.where(half_lane, middle0, pltpu.roll(middle2, NG, 1))
    imag1 = jnp.where(half_lane, pltpu.roll(middle0, NG, 1), middle2)
    real = jnp.concatenate([real0, real1, real2], 1)
    imag = jnp.concatenate([imag0, imag1, imag2], 1)
    right_sum = jnp.concatenate([real, imag], 0).astype(BF16)
    right_cross = jnp.concatenate([imag, -real], 0).astype(BF16)
    for left, rows in ((full, pl.ds(full_row, 128)), (half, pl.ds(half_row, NG))):
        chi_real[rows, :] = -dot(left, right_sum, ((0,), (0,)))
        chi_imag[rows, :] = dot(left, right_cross, ((0,), (0,)))


def product(rows, columns, shape):
    count, width = shape.shape
    out = pl.BlockSpec((count, CHIP_POINTS), lambda side: (0, side))
    return pl.pallas_call(
        product_kernel,
        grid=(width // CHIP_POINTS,),
        out_shape=(shape, shape),
        in_specs=[
            pl.BlockSpec((8, 128, 128), lambda side: (0, 0, 0)),
            pl.BlockSpec((2, 1, 8, 128, 128), lambda side: (0, side, 0, 0, 0)),
        ],
        out_specs=(out, out),
        compiler_params=pltpu.CompilerParams(vmem_limit_bytes=56 * 1024 * 1024),
    )(rows, columns)


def per_device(
    psi_valence,
    psi_conduction,
    energy_valence,
    energy_conduction,
    pair_valence,
    pair_conduction,
    g_index,
):
    def tiles(psi):
        bands = psi.shape[0]
        return psi.reshape(bands, 2, 32, 128).transpose(0, 2, 1, 3).reshape(bands, NG, 128)

    psi_c, psi_v = tiles(psi_conduction), tiles(psi_valence)
    points = g_index.shape[0]
    shape = jax.ShapeDtypeStruct(
        (points // lax.axis_size("fft"), points // lax.axis_size("grp")), F32
    )
    smem = pl.BlockSpec(memory_space=pltpu.SMEM)
    vmem = pl.BlockSpec(memory_space=pltpu.VMEM)
    anywhere = pl.BlockSpec(memory_space=pl.ANY)
    dma = pltpu.SemaphoreType.DMA

    slabs = pltpu.VMEM((CHIPS, 128, 128), jnp.int16)
    blocks = pltpu.VMEM((8, 128, 128), BF16)
    rows, columns = pl.pallas_call(
        functools.partial(kernel, PAIRS * lax.axis_size("grp")),
        out_shape=(
            jax.ShapeDtypeStruct((8, 128, 128), BF16),
            jax.ShapeDtypeStruct((2, 2, 8, 128, 128), BF16),
        ),
        in_specs=[smem] * 4 + [anywhere] * 2 + [vmem] * 4,
        out_specs=(anywhere, anywhere),
        scratch_shapes=[
            pltpu.VMEM(psi_v.shape, BF16),
            *[pltpu.VMEM((psi_c.shape[0], PIECE, 128), BF16)] * LOADS,
            pltpu.VMEM((PAIRS * NG, 128), F32),
            pltpu.VMEM((HALF_C, 128, 128), F32),
            pltpu.VMEM((6 * BOTH, KEYS), FP8),
            pltpu.VMEM((8, points), F32),
            pltpu.VMEM((2, CHIPS, 128, 128), F32),
            pltpu.VMEM((CHIPS, 128, 128), F32),
            pltpu.VMEM((8, 128, 128), F32),
            pltpu.VMEM((8, 128, 128), jnp.int16), pltpu.VMEM((8, 128, 128), jnp.int16),
            slabs, slabs,
            pltpu.VMEM((128, 128), BF16),
            blocks, blocks,
            pltpu.VMEM((2, 2, 8, 128, 128), BF16),
            dma((8 + LOADS,)),
            dma((8,)), dma((8,)),
            dma((CHIPS,)), dma((CHIPS,)), dma((CHIPS,)), dma((CHIPS,)),
            dma((8,)), dma((8,)), dma((8,)), dma((8,)),
            dma((8, 2)), dma((2, 8)), dma((2, 8)), dma((2, 8)),
        ],
        compiler_params=pltpu.CompilerParams(
            collective_id=0, has_side_effects=True, vmem_limit_bytes=62 * 1024 * 1024
        ),
    )(
        pair_conduction, pair_valence, energy_conduction, energy_valence, psi_c, psi_v,
        jnp.asarray(table_z()), jnp.asarray(table_y()), jnp.asarray(table_x()),
        g_index.reshape(1, -1),
    )
    return product(rows, columns, shape)


def solution(mesh):
    placed = (P(None, "fft", None), P(None, "fft", None), P(), P(), P("grp"), P("grp"), P())
    return jax.shard_map(
        per_device,
        mesh=mesh,
        in_specs=placed,
        out_specs=(P("fft", "grp"), P("fft", "grp")),
        check_vma=False,
    )
```
